512 devices in a mesh: chain: 64 (over z, y), rows: 8 (over x, core).
Axes of the slice: x: 4, y: 4, z: 16, core: 2. Of those that a mesh axis runs over, the one named last changes fastest.
Arguments:
- rhs: float32 [512, 32768], P('rows', 'chain'), may hold values from -3 to 3
- diag_factors: float32 [9, 512, 512], P(None, 'rows'), may hold values from -1 to 1
- left_factors: float32 [9, 512, 512], P(None, 'rows'), may hold values from -0.1875 to 0.1875
- right_factors: float32 [9, 512, 512], P(None, 'rows'), may hold values from -0.1875 to 0.1875
Outputs:
- voltages: float32 [512, 32768], P('rows', 'chain')
The draws below stay inside these ranges and needn't reach their ends.
All inputs are finite; a program needn't handle non-finite values.
Results may differ from the reference program's by a relative error of at most 0.00019.
Values sent between devices are 32-bit elements; how exact they have to be, the bound alone decides.
A program may use at most 64 MiB of HBM per device.

```python
import math
import jax
import jax.numpy as jnp
from jax import lax

M = 512
NRHS = 64
LEV = 9
NB = 512


def draw_diag_factors(key, part):
    key = jax.random.fold_in(key, 7)
    diag_key, off_key = jax.random.split(key)
    diag_values = jax.random.uniform(diag_key, (LEV, M, 1), jnp.float32, 0.3, 0.7)
    spread = jnp.clip(jax.random.normal(off_key, (LEV, M, M), jnp.float32), -4.0, 4.0) * (0.3 / math.sqrt(M))
    identity = jnp.eye(M, dtype=jnp.float32)
    return identity * diag_values + (1.0 - identity) * spread


def shard_levels(rng, shape, shards, least, largest):
    def one(axis_at, blocks):
        heights = jax.random.uniform(jax.random.fold_in(jax.random.fold_in(rng, 6), axis_at), (blocks,), jnp.float32, least / len(shards), largest / len(shards))
        return jnp.repeat(jnp.exp(heights), shape[axis_at] // blocks).reshape((-1,) + (1,) * (len(shape) - axis_at - 1))

    level = one(*shards[0])
    for cut in shards[1:]:
        level = level * one(*cut)
    return level


def normal_values(rng, extent, deviation, most, shards=(), kind=jnp.bfloat16):
    factor_of = shard_levels(rng, extent, shards, -0.22, 0.18) if shards else 1.0
    result = jax.random.normal(rng, extent, jnp.float32) * deviation * factor_of
    return jnp.minimum(jnp.maximum(result, -most), most).astype(kind)


def setup_inputs(seed: int = 0) -> dict:
    key_of = jax.random.split(jax.random.key(seed), 5)
    return {
        "rhs": normal_values(key_of[0], (M, NB * NRHS), 0.5, 3.0, ((0, 8), (1, 64)), jnp.float32),
        "diag_factors": draw_diag_factors(jax.random.fold_in(key_of[4], 71), 0),
        "left_factors": normal_values(key_of[2], (LEV, M, M), (2 * M) ** -0.5, 0.1875, ((1, 8),), jnp.float32),
        "right_factors": normal_values(key_of[3], (LEV, M, M), (2 * M) ** -0.5, 0.1875, ((1, 8),), jnp.float32),
    }


def product(matrix, current):
    return jnp.dot(matrix, current, precision=lax.Precision.HIGHEST, preferred_element_type=jnp.float32)


def reference(rhs, diag_factors, left_factors, right_factors):
    current = rhs
    columns = NB * NRHS
    for level in range(LEV):
        cut_cols = (2 ** level) * NRHS
        own_term = product(diag_factors[level], current)
        left_term = product(left_factors[level], current)
        right_term = product(right_factors[level], current)
        left_in = jnp.pad(left_term[:, :columns - cut_cols], ((0, 0), (cut_cols, 0)))
        right_in = jnp.pad(right_term[:, cut_cols:], ((0, 0), (0, cut_cols)))
        current = own_term - left_in - right_in
    return current
```

```python
import functools

import jax
import jax.numpy as jnp
from jax import lax
from jax.experimental import pallas as pl
from jax.experimental.pallas import tpu as pltpu
from jax.sharding import PartitionSpec as P

MESH = pl.DeviceIdType.MESH
F32 = jnp.float32
BF16 = jnp.bfloat16
NX = 4


def shift_down(v, by):
    n, w = v.shape
    if by % 8 == 0:
        return jnp.concatenate((jnp.zeros((by, w), v.dtype), v[: n - by]), axis=0)
    rows = lax.broadcasted_iota(jnp.int32, v.shape, 0)
    return jnp.where(rows < by, 0.0, pltpu.roll(v, by, 0))


def shift_up(v, by):
    n, w = v.shape
    if by % 8 == 0:
        return jnp.concatenate((v[by:], jnp.zeros((by, w), v.dtype)), axis=0)
    rows = lax.broadcasted_iota(jnp.int32, v.shape, 0)
    return jnp.where(rows >= n - by, 0.0, pltpu.roll(v, n - by, 0))


def dot_t(a, b):
    return lax.dot_general(a, b, (((1,), (1,)), ((), ())), preferred_element_type=F32)


def kernel(
    n_chain, levels, groups,
    rhs, diag, left_f, right_f, out,
    x2, src, g0, G, fraw, fhi, flo, ghi, glo, prod, hs, hx, obuf, back, bdst, tb, zb,
    loc_sem, fsend_sem, frecv_sem, pair_send, pair_recv, a2a_send, a2a_recv, ag_send, ag_recv,
):
    C = n_chain
    dev_rows = rhs.shape[0]
    R = 2 * dev_rows
    n_half = src.shape[1]
    Q = C * n_half
    Qs = Q // 2
    hq = Qs // 2
    chain = lax.axis_index("chain")
    rows = lax.axis_index("rows")
    core = lax.rem(rows, 2)
    x = rows // 2
    partner = (chain, x * 2 + (1 - core))
    right = (chain, lax.rem(x + 1, NX) * 2 + core)
    left = (chain, lax.rem(x + NX - 1, NX) * 2 + core)
    facs = (diag, left_f, right_f)

    def local_factor(g, f):
        lo, hi = groups[g]
        return pltpu.make_async_copy(
            facs[f].at[lo:hi], fraw.at[f, lo:hi, core], loc_sem.at[g, f]
        )

    for g in range(len(groups)):
        for f in range(3):
            local_factor(g, f).start()

    barrier = pltpu.get_barrier_semaphore()
    for dev in (partner, right, left):
        pl.semaphore_signal(barrier, inc=1, device_id=dev, device_id_type=MESH)

    def greet(step, carry):
        peer = lax.rem(chain + step, C)
        pl.semaphore_signal(barrier, inc=1, device_id=(peer, rows), device_id_type=MESH)
        return carry

    lax.fori_loop(1, C, greet, 0)
    pl.semaphore_wait(barrier, C - 1 + 3)

    def pair_copy(k, source, target):
        return pltpu.make_async_remote_copy(
            src_ref=source, dst_ref=target, send_sem=pair_send.at[k], recv_sem=pair_recv.at[k],
            device_id=partner, device_id_type=MESH,
        )

    swap = pair_copy(0, rhs, x2.at[core])
    swap.start()

    def remote_factor(g, f):
        lo, hi = groups[g]
        return pltpu.make_async_remote_copy(
            src_ref=facs[f].at[lo:hi], dst_ref=fraw.at[f, lo:hi, core],
            send_sem=fsend_sem.at[g, f], recv_sem=frecv_sem.at[g, f],
            device_id=partner, device_id_type=MESH,
        )

    for g in range(len(groups)):
        for f in range(3):
            remote_factor(g, f).start()

    x2[core] = rhs[...]
    swap.wait()

    for m in range(n_half):
        piece = x2[:, :, m * 2 * C : (m + 1) * 2 * C].reshape(R, 2 * C)
        turned = jnp.transpose(piece)
        src[:, m, :] = jnp.where(core == 0, turned[:C], turned[C:])

    def exchange(k, source, target):
        mine = pltpu.make_async_copy(source.at[chain], target.at[chain], a2a_recv.at[k])
        mine.start()

        def go(step, carry):
            peer = lax.rem(chain + step, C)
            pltpu.make_async_remote_copy(
                src_ref=source.at[peer], dst_ref=target.at[chain],
                send_sem=a2a_send.at[k], recv_sem=a2a_recv.at[k],
                device_id=(peer, rows), device_id_type=MESH,
            ).start()
            return carry

        lax.fori_loop(1, C, go, 0)

    def exchange_wait(k, target):
        pltpu.make_async_copy(target, target, a2a_recv.at[k]).wait()

    def exchange_sent(k, source):
        part = source.at[pl.ds(0, C - 1)]
        pltpu.make_async_copy(part, part, a2a_send.at[k]).wait()

    exchange(0, src, g0)

    def factors_here(g):
        for f in range(3):
            local_factor(g, f).wait()
            remote_factor(g, f).wait_recv()

    def prepare(level):
        for g, (lo, _) in enumerate(groups):
            if lo == level:
                factors_here(g)
        for f in range(3):
            for rel in range(NX):
                at = pl.multiple_of(lax.rem(x + NX - (0, 1, 2, 3)[rel], NX) * R, R)
                v = fraw[f, level, :, :, pl.ds(at, R)].reshape(R, R)
                hi = v.astype(BF16)
                fhi[level, f * R : (f + 1) * R, rel * R : (rel + 1) * R] = hi
                flo[level, f * R : (f + 1) * R, rel * R : (rel + 1) * R] = (v - hi.astype(F32)).astype(BF16)

    halves = (pl.ds(0, hq), pl.ds(hq, hq))

    route = (
        (0, 1, 0, right),
        (0, 3, 1, left),
        (0, 1, 1, right),
        (0, 3, 0, left),
        (1, 2, 0, right),
        (3, 2, 1, left),
    )

    def hop(level, t, k):
        from_slot, to_slot, half, dev = route[k]
        return pltpu.make_async_remote_copy(
            src_ref=G.at[level, t, from_slot, halves[half]],
            dst_ref=G.at[level, t, to_slot, halves[half]],
            send_sem=ag_send.at[level, t], recv_sem=ag_recv.at[level, t, k],
            device_id=dev, device_id_type=MESH,
        )

    def send(level, t):
        for k in range(4):
            hop(level, t, k).start()

    def forward(level, t):
        for k in range(2):
            hop(level, t, k).wait_recv()
            hop(level, t, k + 4).start()

    def sent(level, t):
        part = G.at[level, t, pl.ds(0, 3)]
        pltpu.make_async_copy(part, part, ag_send.at[level, t]).wait()

    def products(level, t):
        for k in (2, 3, 4, 5):
            hop(level, t, k).wait_recv()
        for rel in range(NX):
            v = G[level, t, rel]
            hi = v.astype(BF16)
            ghi[t, :, rel * R : (rel + 1) * R] = hi
            glo[t, :, rel * R : (rel + 1) * R] = (v - hi.astype(F32)).astype(BF16)
        a, b = ghi[t], fhi[level]
        return dot_t(a, b) + dot_t(glo[t], b) + dot_t(a, flo[level])

    prepare(0)
    prepare(1)
    exchange_wait(0, g0)
    for t in range(2):
        for m in range(n_half):
            G[0, t, 0, pl.ds(m, C // 2, stride=n_half), :] = g0[t * (C // 2) : (t + 1) * (C // 2), m, :]
        send(0, t)
    forward(0, 0)
    forward(0, 1)
    for t in range(2):
        prod[t * Qs : (t + 1) * Qs, :] = products(0, t)
    lp = prod[:, R : 2 * R]
    rp = prod[:, 2 * R :]
    hs[...] = jnp.where(core == 0, lp + shift_up(rp, 1), shift_down(lp, 1) + rp)
    other = pair_copy(1, hs, hx)
    other.start()
    prepare(2)
    other.wait()
    new = prod[:, :R] - hx[...]
    for t in range(2):
        G[1, t, 0] = new[t * Qs : (t + 1) * Qs]
        send(1, t)

    prepare(3)
    forward(1, 0)
    forward(1, 1)
    for t in range(2):
        prod[t * Qs : (t + 1) * Qs, :] = products(1, t)
    obuf[...] = prod[:, :R] - shift_down(prod[:, R : 2 * R], 1) - shift_up(prod[:, 2 * R :], 1)
    for t in range(2):
        G[2, t, 0] = obuf[pl.ds(t, Qs, stride=2), :]
        send(2, t)

    def finish(level, t):
        p = products(level, t)
        by = 2 ** (level - 2)
        new = p[:, :R] - shift_down(p[:, R : 2 * R], by) - shift_up(p[:, 2 * R :], by)
        if level + 1 < levels:
            G[level + 1, t, 0] = new
            send(level + 1, t)
        else:
            obuf[t * Qs : (t + 1) * Qs, :] = new
            back[:, t, :] = obuf[pl.ds(t * Qs, C, stride=2), :]
            back[:, 2 + t, :] = obuf[pl.ds(t * Qs + 1, C, stride=2), :]

    forward(2, 0)
    forward(2, 1)
    for level in range(2, levels):
        if level + 2 < levels:
            prepare(level + 2)
        finish(level, 0)
        if level + 1 < levels:
            forward(level + 1, 0)
        finish(level, 1)
        if level + 1 < levels:
            forward(level + 1, 1)

    exchange(1, back, bdst)
    for level in range(levels):
        for t in range(2):
            sent(level, t)
    for g in range(len(groups)):
        for f in range(3):
            remote_factor(g, f).wait_send()
    exchange_sent(0, src)
    exchange_wait(1, bdst)
    for m in range(n_half):
        tb[m] = jnp.transpose(bdst[:, m, :])
    away = pl.ds(pl.multiple_of((1 - core) * dev_rows, dev_rows), dev_rows)
    home = pl.ds(pl.multiple_of(core * dev_rows, dev_rows), dev_rows)
    last = pair_copy(2, tb.at[:, away], zb)
    last.start()
    exchange_sent(1, back)
    last.wait()
    for m in range(n_half):
        own = tb[m, home]
        got = zb[m]
        out[:, m * 2 * C : m * 2 * C + C] = jnp.where(core == 0, own, got)
        out[:, m * 2 * C + C : (m + 1) * 2 * C] = jnp.where(core == 0, got, own)


def solution(mesh):
    n_chain, n_rows = mesh.shape["chain"], mesh.shape["rows"]
    assert n_rows == 2 * NX

    def on_device(rhs, diag, left_f, right_f):
        levels, dev_rows, M = diag.shape
        n_half = rhs.shape[1] // n_chain // 2
        C, R = n_chain, 2 * dev_rows
        Q = C * n_half
        Qs = Q // 2
        groups = ((0, 1), (1, 3), (3, levels))
        scratch = [
            pltpu.VMEM((2,) + rhs.shape, F32),
            pltpu.VMEM((C, n_half, R), F32),
            pltpu.VMEM((C, n_half, R), F32),
            pltpu.VMEM((levels, 2, NX, Qs, R), F32),
            pltpu.VMEM((3, levels, 2, dev_rows, M), F32),
            pltpu.VMEM((levels, 3 * R, M), BF16),
            pltpu.VMEM((levels, 3 * R, M), BF16),
            pltpu.VMEM((2, Qs, M), BF16),
            pltpu.VMEM((2, Qs, M), BF16),
            pltpu.VMEM((Q, 3 * R), F32),
            pltpu.VMEM((Q, R), F32),
            pltpu.VMEM((Q, R), F32),
            pltpu.VMEM((Q, R), F32),
            pltpu.VMEM((C, n_half, R), F32),
            pltpu.VMEM((C, n_half, R), F32),
            pltpu.VMEM((n_half, R, C), F32),
            pltpu.VMEM((n_half, dev_rows, C), F32),
            pltpu.SemaphoreType.DMA((len(groups), 3)),
            pltpu.SemaphoreType.DMA((len(groups), 3)),
            pltpu.SemaphoreType.DMA((len(groups), 3)),
            pltpu.SemaphoreType.DMA((3,)),
            pltpu.SemaphoreType.DMA((3,)),
            pltpu.SemaphoreType.DMA((2,)),
            pltpu.SemaphoreType.DMA((2,)),
            pltpu.SemaphoreType.DMA((levels, 2)),
            pltpu.SemaphoreType.DMA((levels, 2, 6)),
        ]
        vm = pl.BlockSpec(memory_space=pltpu.VMEM)
        hbm = pl.BlockSpec(memory_space=pl.ANY)
        return pl.pallas_call(
            functools.partial(kernel, n_chain, levels, groups),
            out_shape=jax.ShapeDtypeStruct(rhs.shape, F32),
            in_specs=[vm, hbm, hbm, hbm],
            out_specs=vm,
            scratch_shapes=scratch,
            compiler_params=pltpu.CompilerParams(
                collective_id=0, has_side_effects=True, vmem_limit_bytes=48 * 2**20
            ),
        )(rhs, diag, left_f, right_f)

    placed = (
        P("rows", "chain"),
        P(None, "rows", None),
        P(None, "rows", None),
        P(None, "rows", None),
    )
    return jax.shard_map(
        on_device, mesh=mesh, in_specs=placed, out_specs=P("rows", "chain"), check_vma=False
    )
```

```python
import functools

import jax
import jax.numpy as jnp
from jax import lax
from jax.experimental import pallas as pl
from jax.experimental.pallas import tpu as pltpu
from jax.sharding import PartitionSpec as P

MESH = pl.DeviceIdType.MESH
F32 = jnp.float32
BF16 = jnp.bfloat16
NX = 4
NY = 4


def shift_down(v, by):
    n, w = v.shape
    if by % 8 == 0:
        return jnp.concatenate((jnp.zeros((by, w), v.dtype), v[: n - by]), axis=0)
    rows = lax.broadcasted_iota(jnp.int32, v.shape, 0)
    return jnp.where(rows < by, 0.0, pltpu.roll(v, by, 0))


def shift_up(v, by):
    n, w = v.shape
    if by % 8 == 0:
        return jnp.concatenate((v[by:], jnp.zeros((by, w), v.dtype)), axis=0)
    rows = lax.broadcasted_iota(jnp.int32, v.shape, 0)
    return jnp.where(rows >= n - by, 0.0, pltpu.roll(v, n - by, 0))


def dot_t(a, b):
    return lax.dot_general(a, b, (((1,), (1,)), ((), ())), preferred_element_type=F32)


def kernel(
    n_chain, levels, groups,
    rhs, diag, left_f, right_f, out,
    x2, src, ybuf, g0, G, fraw, fhi, flo, ghi, glo, prod, hs, hx, obuf, back, zbuf, bdst, turn, tb, zb,
    loc_sem, fsend_sem, frecv_sem, pair_send, pair_recv, a2a_send, a2a_recv, ag_send, ag_recv, own_sem, known,
):
    C = n_chain
    nz = C // NY
    dev_rows = rhs.shape[0]
    R = 2 * dev_rows
    n_half = src.shape[2]
    Q = C * n_half
    Qs = Q // 2
    chain = lax.axis_index("chain")
    rows = lax.axis_index("rows")
    core = lax.rem(rows, 2)
    x = rows // 2
    y = lax.rem(chain, NY)
    z = chain // NY
    partner = (chain, x * 2 + (1 - core))
    right = (chain, lax.rem(x + 1, NX) * 2 + core)
    left = (chain, lax.rem(x + NX - 1, NX) * 2 + core)
    across = (chain, lax.rem(x + 2, NX) * 2 + core)
    facs = (diag, left_f, right_f)

    def z_of(by):
        return lax.rem(z + by + nz, nz)

    def y_of(by):
        return lax.rem(y + by, NY)

    def z_dev(by):
        return (z_of(by) * NY + y, rows)

    def y_dev(by):
        return (z * NY + y_of(by), rows)

    def both_ways(by):
        return (by,) if 2 * by == nz else (by, -by)

    def signal(sem, dev):
        pl.semaphore_signal(sem, inc=1, device_id=dev, device_id_type=MESH)

    barrier = pltpu.get_barrier_semaphore()
    near = [partner, right, left, across] + [z_dev(b) for b in both_ways(1)] + [y_dev(b) for b in range(1, NY)]
    for dev in near:
        signal(barrier, dev)

    def local_factor(g, f):
        lo, hi = groups[g]
        return pltpu.make_async_copy(
            facs[f].at[lo:hi], fraw.at[f, lo:hi, core], loc_sem.at[g, f]
        )

    own_rhs = pltpu.make_async_copy(rhs, x2.at[core], own_sem)
    own_rhs.start()
    for g in range(len(groups)):
        for f in range(3):
            local_factor(g, f).start()

    pl.semaphore_wait(barrier, len(near))

    def pair_copy(k, source, target):
        return pltpu.make_async_remote_copy(
            src_ref=source, dst_ref=target, send_sem=pair_send.at[k], recv_sem=pair_recv.at[k],
            device_id=partner, device_id_type=MESH,
        )

    swap = pair_copy(0, rhs, x2.at[core])
    swap.start()

    rounds = max(0, nz.bit_length() - 2)

    def tell(k):
        if k < rounds:
            for b in both_ways(2**k):
                signal(known.at[k], z_dev(b))

    def told(k):
        if k < rounds:
            pl.semaphore_wait(known.at[k], len(both_ways(2**k)))

    tell(0)

    def remote_factor(g, f):
        lo, hi = groups[g]
        return pltpu.make_async_remote_copy(
            src_ref=facs[f].at[lo:hi], dst_ref=fraw.at[f, lo:hi, core],
            send_sem=fsend_sem.at[g, f], recv_sem=frecv_sem.at[g, f],
            device_id=partner, device_id_type=MESH,
        )

    for f in range(3):
        remote_factor(0, f).start()

    told(0)
    tell(1)
    own_rhs.wait()
    swap.wait()

    for m in range(n_half):
        piece = x2[:, :, m * 2 * C : (m + 1) * 2 * C].reshape(R, 2 * C)
        turned = jnp.transpose(piece)
        mine = jnp.where(core == 0, turned[:C], turned[C:])
        for cz in range(nz):
            src[cz, :, m, :] = mine[cz * NY : (cz + 1) * NY]

    def phase(k, source, target, mine, others):
        own = pltpu.make_async_copy(source(mine), target.at[mine], a2a_recv.at[k])
        for place, dev in others:
            pltpu.make_async_remote_copy(
                src_ref=source(place), dst_ref=target.at[mine],
                send_sem=a2a_send.at[k], recv_sem=a2a_recv.at[k],
                device_id=dev, device_id_type=MESH,
            ).start()
        own.start()

    def landed(k, target):
        pltpu.make_async_copy(target, target, a2a_recv.at[k]).wait()

    def gone(k, part):
        pltpu.make_async_copy(part, part, a2a_send.at[k]).wait()

    y_others = [(y_of(b), y_dev(b)) for b in range(1, NY)]
    z_others = []
    for b in range(nz // 2, 0, -1):
        for by in both_ways(b):
            z_others.append((z_of(by), z_dev(by)))

    phase(0, lambda p: src.at[:, p], ybuf, y, y_others)
    told(1)
    tell(2)
    for g in range(1, len(groups)):
        for f in range(3):
            remote_factor(g, f).start()
    landed(0, ybuf)
    for k in range(2, rounds):
        told(k)
        tell(k + 1)
    phase(1, lambda p: ybuf.at[:, p], g0, z, z_others)

    def factors_here(g):
        for f in range(3):
            local_factor(g, f).wait()
            remote_factor(g, f).wait_recv()

    def prepare(level):
        for g, (lo, _) in enumerate(groups):
            if lo == level:
                factors_here(g)
        for f in range(3):
            for rel in range(NX):
                at = pl.multiple_of(lax.rem(x + NX - rel, NX) * R, R)
                v = fraw[f, level, :, :, pl.ds(at, R)].reshape(R, R)
                hi = v.astype(BF16)
                fhi[level, f * R : (f + 1) * R, rel * R : (rel + 1) * R] = hi
                flo[level, f * R : (f + 1) * R, rel * R : (rel + 1) * R] = (v - hi.astype(F32)).astype(BF16)

    route = ((2, across), (1, right), (3, left))

    def hop(level, t, k):
        slot, dev = route[k]
        return pltpu.make_async_remote_copy(
            src_ref=G.at[level, t, 0], dst_ref=G.at[level, t, slot],
            send_sem=ag_send.at[level, t], recv_sem=ag_recv.at[level, t, k],
            device_id=dev, device_id_type=MESH,
        )

    def send(level, t):
        for k in range(3):
            hop(level, t, k).start()

    def sent(level, t):
        part = G.at[level, t, pl.ds(0, 3)]
        pltpu.make_async_copy(part, part, ag_send.at[level, t]).wait()

    def part(level, t, first):
        for rel in (first, first + 1):
            v = G[level, t, rel]
            hi = v.astype(BF16)
            ghi[t, :, rel * R : (rel + 1) * R] = hi
            glo[t, :, rel * R : (rel + 1) * R] = (v - hi.astype(F32)).astype(BF16)
        ks = slice(first * R, (first + 2) * R)
        a, b = ghi[t, :, ks], fhi[level, :, ks]
        return dot_t(a, b) + dot_t(glo[t, :, ks], b) + dot_t(a, flo[level, :, ks])

    def early(level, t):
        hop(level, t, 1).wait_recv()
        prod[t * Qs : (t + 1) * Qs, :] = part(level, t, 0)

    def late(level, t):
        for k in (2, 0):
            hop(level, t, k).wait_recv()
        return prod[t * Qs : (t + 1) * Qs, :] + part(level, t, 2)

    def both(level):
        for t in range(2):
            early(level, t)
        for t in range(2):
            prod[t * Qs : (t + 1) * Qs, :] = late(level, t)

    prepare(0)
    landed(1, g0)
    for t in range(2):
        for c in range(C // 2):
            G[0, t, 0, c * n_half : (c + 1) * n_half, :] = g0[(t * (C // 2) + c) // NY, c % NY]
        send(0, t)
    prepare(1)
    both(0)
    lp = prod[:, R : 2 * R]
    rp = prod[:, 2 * R :]
    hs[...] = jnp.where(core == 0, lp + shift_up(rp, 1), shift_down(lp, 1) + rp)
    other = pair_copy(1, hs, hx)
    other.start()
    prepare(2)
    other.wait()
    new = prod[:, :R] - hx[...]
    for t in range(2):
        G[1, t, 0] = new[t * Qs : (t + 1) * Qs]
        send(1, t)

    prepare(3)
    both(1)
    obuf[...] = prod[:, :R] - shift_down(prod[:, R : 2 * R], 1) - shift_up(prod[:, 2 * R :], 1)
    for t in range(2):
        G[2, t, 0] = obuf[pl.ds(t, Qs, stride=2), :]
        send(2, t)

    def finish(level, t):
        early(level, t)
        p = late(level, t)
        by = 2 ** (level - 2)
        new = p[:, :R] - shift_down(p[:, R : 2 * R], by) - shift_up(p[:, 2 * R :], by)
        if level + 1 < levels:
            G[level + 1, t, 0] = new
            send(level + 1, t)
        else:
            obuf[pl.ds(t, Qs, stride=2), :] = new

    for level in range(2, levels):
        if level + 2 < levels:
            prepare(level + 2)
        finish(level, 0)
        finish(level, 1)

    for c in range(C):
        back[c // NY, c % NY] = obuf[c * n_half : (c + 1) * n_half, :]
    phase(2, lambda p: back.at[p], zbuf, z, z_others)
    for level in range(levels):
        for t in range(2):
            sent(level, t)
    for g in range(len(groups)):
        for f in range(3):
            remote_factor(g, f).wait_send()
    gone(0, src.at[:, pl.ds(0, NY - 1)])
    gone(1, ybuf.at[:, pl.ds(0, nz - 1)])
    landed(2, zbuf)
    phase(3, lambda p: zbuf.at[:, p], bdst, y, y_others)
    gone(2, back.at[pl.ds(0, nz - 1)])
    landed(3, bdst)
    for m in range(n_half):
        for cy in range(NY):
            turn[m, pl.ds(cy, nz, stride=NY), :] = bdst[cy, :, m, :]
        tb[m] = jnp.transpose(turn[m])
    away = pl.ds(pl.multiple_of((1 - core) * dev_rows, dev_rows), dev_rows)
    home = pl.ds(pl.multiple_of(core * dev_rows, dev_rows), dev_rows)
    last = pair_copy(2, tb.at[:, away], zb)
    last.start()
    gone(3, zbuf.at[:, pl.ds(0, NY - 1)])
    last.wait()
    for m in range(n_half):
        own = tb[m, home]
        got = zb[m]
        out[:, m * 2 * C : m * 2 * C + C] = jnp.where(core == 0, own, got)
        out[:, m * 2 * C + C : (m + 1) * 2 * C] = jnp.where(core == 0, got, own)


def solution(mesh):
    n_chain, n_rows = mesh.shape["chain"], mesh.shape["rows"]
    assert n_rows == 2 * NX and n_chain % NY == 0

    def on_device(rhs, diag, left_f, right_f):
        levels, dev_rows, M = diag.shape
        n_half = rhs.shape[1] // n_chain // 2
        C, R = n_chain, 2 * dev_rows
        nz = C // NY
        Q = C * n_half
        Qs = Q // 2
        groups = ((0, 1), (1, 3), (3, levels))
        scratch = [
            pltpu.VMEM((2,) + rhs.shape, F32),
            pltpu.VMEM((nz, NY, n_half, R), F32),
            pltpu.VMEM((NY, nz, n_half, R), F32),
            pltpu.VMEM((nz, NY, n_half, R), F32),
            pltpu.VMEM((levels, 2, NX, Qs, R), F32),
            pltpu.VMEM((3, levels, 2, dev_rows, M), F32),
            pltpu.VMEM((levels, 3 * R, M), BF16),
            pltpu.VMEM((levels, 3 * R, M), BF16),
            pltpu.VMEM((2, Qs, M), BF16),
            pltpu.VMEM((2, Qs, M), BF16),
            pltpu.VMEM((Q, 3 * R), F32),
            pltpu.VMEM((Q, R), F32),
            pltpu.VMEM((Q, R), F32),
            pltpu.VMEM((Q, R), F32),
            pltpu.VMEM((nz, NY, n_half, R), F32),
            pltpu.VMEM((nz, NY, n_half, R), F32),
            pltpu.VMEM((NY, nz, n_half, R), F32),
            pltpu.VMEM((n_half, C, R), F32),
            pltpu.VMEM((n_half, R, C), F32),
            pltpu.VMEM((n_half, dev_rows, C), F32),
            pltpu.SemaphoreType.DMA((len(groups), 3)),
            pltpu.SemaphoreType.DMA((len(groups), 3)),
            pltpu.SemaphoreType.DMA((len(groups), 3)),
            pltpu.SemaphoreType.DMA((3,)),
            pltpu.SemaphoreType.DMA((3,)),
            pltpu.SemaphoreType.DMA((4,)),
            pltpu.SemaphoreType.DMA((4,)),
            pltpu.SemaphoreType.DMA((levels, 2)),
            pltpu.SemaphoreType.DMA((levels, 2, 3)),
            pltpu.SemaphoreType.DMA,
            pltpu.SemaphoreType.REGULAR((3,)),
        ]
        vm = pl.BlockSpec(memory_space=pltpu.VMEM)
        hbm = pl.BlockSpec(memory_space=pl.ANY)
        return pl.pallas_call(
            functools.partial(kernel, n_chain, levels, groups),
            out_shape=jax.ShapeDtypeStruct(rhs.shape, F32),
            in_specs=[hbm, hbm, hbm, hbm],
            out_specs=vm,
            scratch_shapes=scratch,
            compiler_params=pltpu.CompilerParams(
                collective_id=0, has_side_effects=True, vmem_limit_bytes=63 * 2**20
            ),
        )(rhs, diag, left_f, right_f)

    placed = (
        P("rows", "chain"),
        P(None, "rows", None),
        P(None, "rows", None),
        P(None, "rows", None),
    )
    return jax.shard_map(
        on_device, mesh=mesh, in_specs=placed, out_specs=P("rows", "chain"), check_vma=False
    )
```

```python
import functools

import jax
import jax.numpy as jnp
from jax import lax
from jax.experimental import pallas as pl
from jax.experimental.pallas import tpu as pltpu
from jax.sharding import PartitionSpec as P

MESH = pl.DeviceIdType.MESH
F32 = jnp.float32
BF16 = jnp.bfloat16
NX = 4
NY = 4
HALO = 8


def shift_down(v, by):
    n, w = v.shape
    if by % 8 == 0:
        return jnp.concatenate((jnp.zeros((by, w), v.dtype), v[: n - by]), axis=0)
    rows = lax.broadcasted_iota(jnp.int32, v.shape, 0)
    return jnp.where(rows < by, 0.0, pltpu.roll(v, by, 0))


def shift_up(v, by):
    n, w = v.shape
    if by % 8 == 0:
        return jnp.concatenate((v[by:], jnp.zeros((by, w), v.dtype)), axis=0)
    rows = lax.broadcasted_iota(jnp.int32, v.shape, 0)
    return jnp.where(rows >= n - by, 0.0, pltpu.roll(v, n - by, 0))


def dot_t(a, b):
    return lax.dot_general(a, b, (((1,), (1,)), ((), ())), preferred_element_type=F32)


def three_pass(v, f_hi, f_lo):
    hi = v.astype(BF16)
    lo = (v - hi.astype(F32)).astype(BF16)
    return dot_t(hi, f_hi) + dot_t(lo, f_hi) + dot_t(hi, f_lo)


def kernel(
    n_chain, levels, groups,
    rhs, diag, left_f, right_f, out,
    x2, src, ybuf, g0, GN, G, fraw, f0hi, f0lo, fhi, flo, ghi, glo, prod, hs, hx, obuf, es, ex, back, zbuf, bdst, turn,
    loc_sem, fsend_sem, frecv_sem, pair_send, pair_recv, a2a_send, a2a_recv, ag_send, ag_recv, l2_recv, own_sem, known,
):
    C = n_chain
    nz = C // NY
    dev_rows = rhs.shape[0]
    R = 2 * dev_rows
    n_half = src.shape[2]
    Q = C * n_half
    Qs = Q // 2
    Qh = Qs + HALO
    chain = lax.axis_index("chain")
    rows = lax.axis_index("rows")
    core = lax.rem(rows, 2)
    x = rows // 2
    y = lax.rem(chain, NY)
    z = chain // NY
    partner = (chain, x * 2 + (1 - core))
    right = (chain, lax.rem(x + 1, NX) * 2 + core)
    left = (chain, lax.rem(x + NX - 1, NX) * 2 + core)
    across = (chain, lax.rem(x + 2, NX) * 2 + core)
    facs = (diag, left_f, right_f)

    def z_of(by):
        return lax.rem(z + by + nz, nz)

    def y_of(by):
        return lax.rem(y + by, NY)

    def z_dev(by):
        return (z_of(by) * NY + y, rows)

    def y_dev(by):
        return (z * NY + y_of(by), rows)

    def both_ways(by):
        return (by,) if 2 * by == nz else (by, -by)

    def signal(sem, dev):
        pl.semaphore_signal(sem, inc=1, device_id=dev, device_id_type=MESH)

    barrier = pltpu.get_barrier_semaphore()
    reach = min(4, nz // 2)
    near = [z_dev(by) for b in range(reach, 0, -1) for by in both_ways(b)]
    near += [y_dev(b) for b in range(1, NY)] + [across, right, left, partner]
    for dev in near:
        signal(barrier, dev)

    def local_factor(g, f):
        lo, hi = groups[g]
        return pltpu.make_async_copy(
            facs[f].at[lo:hi], fraw.at[f, lo:hi, core], loc_sem.at[g, f]
        )

    own_rhs = pltpu.make_async_copy(rhs, x2, own_sem)
    own_rhs.start()
    for g in range(len(groups)):
        for f in range(3):
            local_factor(g, f).start()

    own_rhs.wait()
    for m in range(n_half):
        turned = jnp.transpose(x2[:, m * 2 * C : (m + 1) * 2 * C])
        pairs = jnp.concatenate((turned[:C], turned[C:]), axis=1)
        for cz in range(nz):
            src[cz, :, m, :] = pairs[cz * NY : (cz + 1) * NY]

    pl.semaphore_wait(barrier, len(near))

    far = nz // 2 > reach
    if far:
        for by in both_ways(reach):
            signal(known, z_dev(by))

    def pair_copy(k, source, target):
        return pltpu.make_async_remote_copy(
            src_ref=source, dst_ref=target, send_sem=pair_send.at[k], recv_sem=pair_recv.at[k],
            device_id=partner, device_id_type=MESH,
        )

    def remote_factor(g, f):
        lo, hi = groups[g]
        return pltpu.make_async_remote_copy(
            src_ref=facs[f].at[lo:hi], dst_ref=fraw.at[f, lo:hi, core],
            send_sem=fsend_sem.at[g, f], recv_sem=frecv_sem.at[g, f],
            device_id=partner, device_id_type=MESH,
        )

    def phase(k, source, target, mine, others):
        own = pltpu.make_async_copy(source(mine), target.at[mine], a2a_recv.at[k])
        for place, dev in others:
            pltpu.make_async_remote_copy(
                src_ref=source(place), dst_ref=target.at[mine],
                send_sem=a2a_send.at[k], recv_sem=a2a_recv.at[k],
                device_id=dev, device_id_type=MESH,
            ).start()
        own.start()

    def landed(k, target):
        pltpu.make_async_copy(target, target, a2a_recv.at[k]).wait()

    def gone(k, part):
        pltpu.make_async_copy(part, part, a2a_send.at[k]).wait()

    y_others = [(y_of(b), y_dev(b)) for b in range(1, NY)]
    z_others = []
    for b in range(nz // 2, 0, -1):
        for by in both_ways(b):
            z_others.append((z_of(by), z_dev(by)))

    phase(0, lambda p: src.at[:, p], ybuf, y, y_others)
    for g in range(len(groups)):
        for f in range(3):
            remote_factor(g, f).start()
    landed(0, ybuf)
    if far:
        pl.semaphore_wait(known, 2)
    phase(1, lambda p: ybuf.at[:, p], g0, z, z_others)

    def factors_here(level):
        for g, (lo, _) in enumerate(groups):
            if lo == level:
                for f in range(3):
                    local_factor(g, f).wait()
                    remote_factor(g, f).wait_recv()

    def columns(f, level, rel):
        at = pl.multiple_of(lax.rem(x + NX - rel, NX) * R, R)
        return fraw[f, level, :, :, pl.ds(at, R)].reshape(R, R)

    def prepare(level):
        factors_here(level)
        for f in range(3):
            for rel in range(NX):
                v = columns(f, level, rel)
                hi = v.astype(BF16)
                fhi[level, f * R : (f + 1) * R, rel * R : (rel + 1) * R] = hi
                flo[level, f * R : (f + 1) * R, rel * R : (rel + 1) * R] = (v - hi.astype(F32)).astype(BF16)

    def low(v):
        return lax.broadcasted_iota(jnp.int32, v.shape, 1) < dev_rows

    def turn_lanes(v):
        return pltpu.roll(v, dev_rows, 1)

    def firsts(a, b):
        return jnp.where(low(a), a, turn_lanes(b))

    def seconds(a, b):
        return jnp.where(low(a), turn_lanes(a), b)

    def prepare_first():
        factors_here(0)
        for f in range(3):
            for k in range(NX // 2):
                a, b = columns(f, 0, 2 * k), columns(f, 0, 2 * k + 1)
                v = jnp.where(core == 0, firsts(a, b), seconds(a, b))
                hi = v.astype(BF16)
                f0hi[f * R : (f + 1) * R, k * R : (k + 1) * R] = hi
                f0lo[f * R : (f + 1) * R, k * R : (k + 1) * R] = (v - hi.astype(F32)).astype(BF16)

    route = ((2, across), (1, right), (3, left))

    def chunk(level, t, slot):
        return GN.at[level, t, slot] if level < 2 else G.at[level - 2, t, slot]

    def hop(level, t, k, piece=None):
        slot, dev = route[k]
        source, target, recv = chunk(level, t, 0), chunk(level, t, slot), ag_recv.at[level, t, k]
        if piece is not None:
            some = pl.ds(piece * (Qs // 2), Qs // 2)
            source, target, recv = source.at[some], target.at[some], l2_recv.at[t, piece, k]
        return pltpu.make_async_remote_copy(
            src_ref=source, dst_ref=target, send_sem=ag_send.at[level, t], recv_sem=recv,
            device_id=dev, device_id_type=MESH,
        )

    def send(level, t, piece=None):
        for k in range(3):
            hop(level, t, k, piece).start()

    def arrived(level, t, k):
        if level == 2:
            for piece in range(2):
                hop(level, t, k, piece).wait_recv()
        else:
            hop(level, t, k).wait_recv()

    def sent(level, t):
        part = chunk(level, t, pl.ds(0, 3))
        pltpu.make_async_copy(part, part, ag_send.at[level, t]).wait()

    def padded(v):
        return jnp.concatenate((v, jnp.zeros((HALO, v.shape[1]), F32)), axis=0)

    prepare_first()
    landed(1, g0)
    first = (0, (Qs - HALO) // n_half)
    for t in range(2):
        for i in range(Qh // n_half):
            c = first[t] + i
            GN[0, t, 0, i * n_half : (i + 1) * n_half, :] = g0[c // NY, c % NY]
        send(0, t)
    prepare(1)
    for t in range(2):
        for k in (1, 2, 0):
            arrived(0, t, k)
        a = [GN[0, t, rel] for rel in range(NX)]
        ev = jnp.concatenate((firsts(a[0], a[1]), firsts(a[2], a[3])), axis=1)
        pe = three_pass(padded(ev), f0hi[...], f0lo[...])[:Qh]
        od = jnp.concatenate((seconds(a[0], a[1]), seconds(a[2], a[3])), axis=1)
        po = three_pass(padded(od), f0hi[...], f0lo[...])[:Qh]
        to_even = pe[:, :R] - shift_down(po[:, R : 2 * R], 1) - po[:, 2 * R :]
        to_odd = po[:, :R] - pe[:, R : 2 * R] - shift_up(pe[:, 2 * R :], 1)
        hs[t] = jnp.where(core == 0, to_odd, to_even)
        other = pair_copy(t, hs.at[t], hx.at[t])
        other.start()
        mine = jnp.where(core == 0, to_even, to_odd)
        other.wait_recv()
        GN[1, t, 0] = mine + hx[t]
        send(1, t)

    prepare(2)
    for t in range(2):
        for k in (1, 2, 0):
            arrived(1, t, k)
        v = jnp.concatenate([GN[1, t, rel] for rel in range(NX)], axis=1)
        p = three_pass(padded(v), fhi[1], flo[1])[:Qh]
        new = p[:, :R] - shift_down(p[:, R : 2 * R], 1) - shift_up(p[:, 2 * R :], 1)
        obuf[t] = new[:Qs] if t == 0 else new[HALO:]
        for u in range(2):
            G[0, u, 0, t * (Qs // 2) : (t + 1) * (Qs // 2), :] = obuf[t, pl.ds(u, Qs // 2, stride=2), :]
            send(2, u, t)

    def part(level, t, first):
        for rel in (first, first + 1):
            v = G[level - 2, t, rel]
            hi = v.astype(BF16)
            ghi[t, :, rel * R : (rel + 1) * R] = hi
            glo[t, :, rel * R : (rel + 1) * R] = (v - hi.astype(F32)).astype(BF16)
        ks = slice(first * R, (first + 2) * R)
        a, b = ghi[t, :, ks], fhi[level, :, ks]
        return dot_t(a, b) + dot_t(glo[t, :, ks], b) + dot_t(a, flo[level, :, ks])

    def finish(level, t):
        arrived(level, t, 1)
        prod[t] = part(level, t, 0)
        arrived(level, t, 2)
        arrived(level, t, 0)
        p = prod[t] + part(level, t, 2)
        by = 2 ** (level - 2)
        return p[:, :R] - shift_down(p[:, R : 2 * R], by) - shift_up(p[:, 2 * R :], by)

    for level in range(2, levels - 1):
        prepare(level + 1)
        for t in range(2):
            G[level - 1, t, 0] = finish(level, t)
            send(level + 1, t)

    for t in range(2):
        new = finish(levels - 1, t)
        es[t] = new
        other = pair_copy(2 + t, es.at[t], ex.at[t])
        other.start()
        other.wait_recv()
        got = turn_lanes(ex[t])
        both = jnp.where(low(new) == (core == 0), new, got)
        for c in range(C):
            back[t, c // NY, c % NY] = both[2 * c : 2 * c + 2]
        phase(2 + t, lambda p: back.at[t, p], zbuf.at[t], z, z_others)

    for level in range(levels):
        for t in range(2):
            sent(level, t)
    for g in range(len(groups)):
        for f in range(3):
            remote_factor(g, f).wait_send()
    gone(0, src.at[:, pl.ds(0, NY - 1)])
    gone(1, ybuf.at[:, pl.ds(0, nz - 1)])
    for t in range(2):
        pair_copy(t, hs.at[t], hx.at[t]).wait_send()
        pair_copy(2 + t, es.at[t], ex.at[t]).wait_send()
    for t in range(2):
        landed(2 + t, zbuf.at[t])
        phase(4 + t, lambda p: zbuf.at[t, :, p], bdst.at[t], y, y_others)
    for t in range(2):
        gone(2 + t, back.at[t, pl.ds(0, nz - 1)])
        landed(4 + t, bdst.at[t])
        for j in range(2):
            m = 2 * j + t
            for cy in range(NY):
                turn[m, pl.ds(cy, nz, stride=NY), :] = bdst[t, cy, :, j, :]
            wide = jnp.transpose(turn[m])
            out[:, m * 2 * C : (m + 1) * 2 * C] = jnp.concatenate((wide[:dev_rows], wide[dev_rows:]), axis=1)
    for t in range(2):
        gone(4 + t, zbuf.at[t, :, pl.ds(0, NY - 1)])


def solution(mesh):
    n_chain, n_rows = mesh.shape["chain"], mesh.shape["rows"]
    assert n_rows == 2 * NX and n_chain % NY == 0

    def on_device(rhs, diag, left_f, right_f):
        levels, dev_rows, M = diag.shape
        n_half = rhs.shape[1] // n_chain // 2
        C, R = n_chain, 2 * dev_rows
        nz = C // NY
        Q = C * n_half
        Qs = Q // 2
        Qh = Qs + HALO
        groups = ((0, 1), (1, 3), (3, levels))
        scratch = [
            pltpu.VMEM(rhs.shape, F32),
            pltpu.VMEM((nz, NY, n_half, R), F32),
            pltpu.VMEM((NY, nz, n_half, R), F32),
            pltpu.VMEM((nz, NY, n_half, R), F32),
            pltpu.VMEM((2, 2, NX, Qh, R), F32),
            pltpu.VMEM((levels - 2, 2, NX, Qs, R), F32),
            pltpu.VMEM((3, levels, 2, dev_rows, M), F32),
            pltpu.VMEM((3 * R, M // 2), BF16),
            pltpu.VMEM((3 * R, M // 2), BF16),
            pltpu.VMEM((levels, 3 * R, M), BF16),
            pltpu.VMEM((levels, 3 * R, M), BF16),
            pltpu.VMEM((2, Qs, M), BF16),
            pltpu.VMEM((2, Qs, M), BF16),
            pltpu.VMEM((2, Qs, 3 * R), F32),
            pltpu.VMEM((2, Qh, R), F32),
            pltpu.VMEM((2, Qh, R), F32),
            pltpu.VMEM((2, Qs, R), F32),
            pltpu.VMEM((2, Qs, R), F32),
            pltpu.VMEM((2, Qs, R), F32),
            pltpu.VMEM((2, nz, NY, 2, R), F32),
            pltpu.VMEM((2, nz, NY, 2, R), F32),
            pltpu.VMEM((2, NY, nz, 2, R), F32),
            pltpu.VMEM((n_half, C, R), F32),
            pltpu.SemaphoreType.DMA((len(groups), 3)),
            pltpu.SemaphoreType.DMA((len(groups), 3)),
            pltpu.SemaphoreType.DMA((len(groups), 3)),
            pltpu.SemaphoreType.DMA((4,)),
            pltpu.SemaphoreType.DMA((4,)),
            pltpu.SemaphoreType.DMA((6,)),
            pltpu.SemaphoreType.DMA((6,)),
            pltpu.SemaphoreType.DMA((levels, 2)),
            pltpu.SemaphoreType.DMA((levels, 2, 3)),
            pltpu.SemaphoreType.DMA((2, 2, 3)),
            pltpu.SemaphoreType.DMA,
            pltpu.SemaphoreType.REGULAR,
        ]
        vm = pl.BlockSpec(memory_space=pltpu.VMEM)
        hbm = pl.BlockSpec(memory_space=pl.ANY)
        return pl.pallas_call(
            functools.partial(kernel, n_chain, levels, groups),
            out_shape=jax.ShapeDtypeStruct(rhs.shape, F32),
            in_specs=[hbm, hbm, hbm, hbm],
            out_specs=vm,
            scratch_shapes=scratch,
            compiler_params=pltpu.CompilerParams(
                collective_id=0, has_side_effects=True, vmem_limit_bytes=215 * 2**18
            ),
        )(rhs, diag, left_f, right_f)

    placed = (
        P("rows", "chain"),
        P(None, "rows", None),
        P(None, "rows", None),
        P(None, "rows", None),
    )
    return jax.shard_map(
        on_device, mesh=mesh, in_specs=placed, out_specs=P("rows", "chain"), check_vma=False
    )
```

```python
import functools

import jax
import jax.numpy as jnp
from jax import lax
from jax.experimental import pallas as pl
from jax.experimental.pallas import tpu as pltpu
from jax.sharding import PartitionSpec as P

MESH = pl.DeviceIdType.MESH
F32 = jnp.float32
BF16 = jnp.bfloat16
NX = 4
NY = 4
HALO = 8
ORDER = (0, 2, 1, 3)


def shift_down(v, by):
    n, w = v.shape
    if by % 8 == 0:
        return jnp.concatenate((jnp.zeros((by, w), v.dtype), v[: n - by]), axis=0)
    rows = lax.broadcasted_iota(jnp.int32, v.shape, 0)
    return jnp.where(rows < by, 0.0, pltpu.roll(v, by, 0))


def shift_up(v, by):
    n, w = v.shape
    if by % 8 == 0:
        return jnp.concatenate((v[by:], jnp.zeros((by, w), v.dtype)), axis=0)
    rows = lax.broadcasted_iota(jnp.int32, v.shape, 0)
    return jnp.where(rows >= n - by, 0.0, pltpu.roll(v, n - by, 0))


def dot_t(a, b):
    return lax.dot_general(a, b, (((1,), (1,)), ((), ())), preferred_element_type=F32)


def three_pass(v, f_hi, f_lo):
    hi = v.astype(BF16)
    lo = (v - hi.astype(F32)).astype(BF16)
    return dot_t(hi, f_hi) + dot_t(lo, f_hi) + dot_t(hi, f_lo)


def kernel(
    n_chain, levels, groups,
    rhs, diag, left_f, right_f, out,
    x2, src, ybuf, g0, GN, G2, G, fraw, f0hi, f0lo, fhi, flo, ghi, glo, prod, first_half, hs, hx, obuf, es, ex, back, zbuf, bdst, turn,
    loc_sem, fsend_sem, frecv_sem, pair_send, pair_recv, a2a_send, a2a_recv, ag_send, ag_recv, l2_recv, own_sem, known,
):
    C = n_chain
    nz = C // NY
    dev_rows = rhs.shape[0]
    R = 2 * dev_rows
    n_half = src.shape[2]
    Q = C * n_half
    Qs = Q // 2
    Qh = Qs + HALO
    chain = lax.axis_index("chain")
    rows = lax.axis_index("rows")
    core = lax.rem(rows, 2)
    x = rows // 2
    y = lax.rem(chain, NY)
    z = chain // NY
    partner = (chain, x * 2 + (1 - core))
    right = (chain, lax.rem(x + 1, NX) * 2 + core)
    left = (chain, lax.rem(x + NX - 1, NX) * 2 + core)
    across = (chain, lax.rem(x + 2, NX) * 2 + core)
    facs = (diag, left_f, right_f)

    def z_of(by):
        return lax.rem(z + by + nz, nz)

    def y_of(by):
        return lax.rem(y + by, NY)

    def z_dev(by):
        return (z_of(by) * NY + y, rows)

    def y_dev(by):
        return (z * NY + y_of(by), rows)

    def both_ways(by):
        return (by,) if 2 * by == nz else (by, -by)

    def signal(sem, dev):
        pl.semaphore_signal(sem, inc=1, device_id=dev, device_id_type=MESH)

    barrier = pltpu.get_barrier_semaphore()
    reach = min(4, nz // 2)
    near = [z_dev(by) for b in range(reach, 0, -1) for by in both_ways(b)]
    near += [y_dev(b) for b in range(1, NY)] + [across, right, left, partner]
    for dev in near:
        signal(barrier, dev)

    def local_factor(g, f):
        lo, hi = groups[g]
        return pltpu.make_async_copy(
            facs[f].at[lo:hi], fraw.at[f, lo:hi, core], loc_sem.at[g, f]
        )

    own_rhs = pltpu.make_async_copy(rhs, x2, own_sem)
    own_rhs.start()
    for g in range(len(groups)):
        for f in range(3):
            local_factor(g, f).start()

    own_rhs.wait()
    for m in range(n_half):
        turned = jnp.transpose(x2[:, m * 2 * C : (m + 1) * 2 * C])
        pairs = jnp.concatenate((turned[:C], turned[C:]), axis=1)
        for cz in range(nz):
            src[cz, :, m, :] = pairs[cz * NY : (cz + 1) * NY]

    pl.semaphore_wait(barrier, len(near))

    far = nz // 2 > reach
    if far:
        for by in both_ways(reach):
            signal(known, z_dev(by))

    def pair_copy(k, source, target):
        return pltpu.make_async_remote_copy(
            src_ref=source, dst_ref=target, send_sem=pair_send.at[k], recv_sem=pair_recv.at[k],
            device_id=partner, device_id_type=MESH,
        )

    def remote_factor(g, f):
        lo, hi = groups[g]
        return pltpu.make_async_remote_copy(
            src_ref=facs[f].at[lo:hi], dst_ref=fraw.at[f, lo:hi, core],
            send_sem=fsend_sem.at[g, f], recv_sem=frecv_sem.at[g, f],
            device_id=partner, device_id_type=MESH,
        )

    def phase(k, source, target, mine, others):
        own = pltpu.make_async_copy(source(mine), target.at[mine], a2a_recv.at[k])
        for place, dev in others:
            pltpu.make_async_remote_copy(
                src_ref=source(place), dst_ref=target.at[mine],
                send_sem=a2a_send.at[k], recv_sem=a2a_recv.at[k],
                device_id=dev, device_id_type=MESH,
            ).start()
        own.start()

    def landed(k, target):
        pltpu.make_async_copy(target, target, a2a_recv.at[k]).wait()

    def gone(k, part):
        pltpu.make_async_copy(part, part, a2a_send.at[k]).wait()

    y_others = [(y_of(b), y_dev(b)) for b in range(1, NY)]
    z_others = []
    for b in range(nz // 2, 0, -1):
        for by in both_ways(b):
            z_others.append((z_of(by), z_dev(by)))

    phase(0, lambda p: src.at[:, p], ybuf, y, y_others)
    for g in range(len(groups)):
        for f in range(3):
            remote_factor(g, f).start()
    landed(0, ybuf)
    if far:
        pl.semaphore_wait(known, 2)
    phase(1, lambda p: ybuf.at[:, p], g0, z, z_others)

    def factors_here(level):
        for g, (lo, _) in enumerate(groups):
            if lo == level:
                for f in range(3):
                    local_factor(g, f).wait()
                    remote_factor(g, f).wait_recv()

    def columns(f, level, slot):
        at = pl.multiple_of(lax.rem(x + NX - ORDER[slot], NX) * R, R)
        return fraw[f, level, :, :, pl.ds(at, R)].reshape(R, R)

    def prepare(level):
        factors_here(level)
        for f in range(3):
            for rel in range(NX):
                v = columns(f, level, rel)
                hi = v.astype(BF16)
                fhi[level, f * R : (f + 1) * R, rel * R : (rel + 1) * R] = hi
                flo[level, f * R : (f + 1) * R, rel * R : (rel + 1) * R] = (v - hi.astype(F32)).astype(BF16)

    def low(v):
        return lax.broadcasted_iota(jnp.int32, v.shape, 1) < dev_rows

    def turn_lanes(v):
        return pltpu.roll(v, dev_rows, 1)

    def firsts(a, b):
        return jnp.where(low(a), a, turn_lanes(b))

    def seconds(a, b):
        return jnp.where(low(a), turn_lanes(a), b)

    def prepare_first():
        factors_here(0)
        for f in range(3):
            for k in range(NX // 2):
                a, b = columns(f, 0, 2 * k), columns(f, 0, 2 * k + 1)
                v = jnp.where(core == 0, firsts(a, b), seconds(a, b))
                hi = v.astype(BF16)
                f0hi[f * R : (f + 1) * R, k * R : (k + 1) * R] = hi
                f0lo[f * R : (f + 1) * R, k * R : (k + 1) * R] = (v - hi.astype(F32)).astype(BF16)

    route = ((1, across), (2, right), (3, left))

    def chunk(level, t, slot):
        if level < 2:
            return GN.at[level, t, slot]
        return G2.at[t, slot] if level == 2 else G.at[level - 3, t, slot]

    def hop(level, t, k, piece=None):
        slot, dev = route[k]
        source, target, recv = chunk(level, t, 0), chunk(level, t, slot), ag_recv.at[level, t, k]
        if piece is not None:
            some = pl.ds(piece * (Qs // 2), Qs // 2)
            source, target, recv = source.at[some], target.at[some], l2_recv.at[t, piece, k]
        return pltpu.make_async_remote_copy(
            src_ref=source, dst_ref=target, send_sem=ag_send.at[level, t], recv_sem=recv,
            device_id=dev, device_id_type=MESH,
        )

    def send(level, t, piece=None):
        for k in range(3):
            hop(level, t, k, piece).start()

    def arrived(level, t, k):
        if level == 2:
            for piece in range(2):
                hop(level, t, k, piece).wait_recv()
        else:
            hop(level, t, k).wait_recv()

    def sent(level, t):
        part = chunk(level, t, pl.ds(0, 3))
        pltpu.make_async_copy(part, part, ag_send.at[level, t]).wait()

    def padded(v):
        return jnp.concatenate((v, jnp.zeros((HALO, v.shape[1]), F32)), axis=0)

    prepare_first()
    landed(1, g0)
    first = (0, (Qs - HALO) // n_half)
    for t in range(2):
        for i in range(Qh // n_half):
            c = first[t] + i
            GN[0, t, 0, i * n_half : (i + 1) * n_half, :] = g0[c // NY, c % NY]
        send(0, t)
    prepare(1)
    for t in range(2):
        for k in (1, 2, 0):
            arrived(0, t, k)
        a = [GN[0, t, rel] for rel in range(NX)]
        ev = jnp.concatenate((firsts(a[0], a[1]), firsts(a[2], a[3])), axis=1)
        pe = three_pass(padded(ev), f0hi[...], f0lo[...])[:Qh]
        od = jnp.concatenate((seconds(a[0], a[1]), seconds(a[2], a[3])), axis=1)
        po = three_pass(padded(od), f0hi[...], f0lo[...])[:Qh]
        to_even = pe[:, :R] - shift_down(po[:, R : 2 * R], 1) - po[:, 2 * R :]
        to_odd = po[:, :R] - pe[:, R : 2 * R] - shift_up(pe[:, 2 * R :], 1)
        hs[t] = jnp.where(core == 0, to_odd, to_even)
        other = pair_copy(t, hs.at[t], hx.at[t])
        other.start()
        mine = jnp.where(core == 0, to_even, to_odd)
        other.wait_recv()
        GN[1, t, 0] = mine + hx[t]
        send(1, t)

    prepare(2)
    for t in range(2):
        arrived(1, t, 0)
        v = padded(jnp.concatenate((GN[1, t, 0], GN[1, t, 1]), axis=1))
        first_half[...] = three_pass(v, fhi[1, :, : 2 * R], flo[1, :, : 2 * R])[:Qh]
        arrived(1, t, 1)
        arrived(1, t, 2)
        v = padded(jnp.concatenate((GN[1, t, 2], GN[1, t, 3]), axis=1))
        p = first_half[...] + three_pass(v, fhi[1, :, 2 * R :], flo[1, :, 2 * R :])[:Qh]
        new = p[:, :R] - shift_down(p[:, R : 2 * R], 1) - shift_up(p[:, 2 * R :], 1)
        obuf[t] = new[:Qs] if t == 0 else new[HALO:]
        for u in range(2):
            G2[u, 0, t * (Qs // 2) : (t + 1) * (Qs // 2), :] = obuf[t, pl.ds(u, Qs // 2, stride=2), :]
            send(2, u, t)

    def part(level, t, first):
        n = Qs if level == 2 else Qs // 2
        for slot in (first, first + 1):
            v = chunk(level, t, slot)[...]
            hi = v.astype(BF16)
            ghi[t, :n, slot * R : (slot + 1) * R] = hi
            glo[t, :n, slot * R : (slot + 1) * R] = (v - hi.astype(F32)).astype(BF16)
        ks = slice(first * R, (first + 2) * R)
        a, b = ghi[t, :n, ks], fhi[level, :, ks]
        return dot_t(a, b) + dot_t(glo[t, :n, ks], b) + dot_t(a, flo[level, :, ks])

    def finish(level, t):
        n = Qs if level == 2 else Qs // 2
        arrived(level, t, 0)
        prod[t, :n] = part(level, t, 0)
        arrived(level, t, 1)
        arrived(level, t, 2)
        p = prod[t, :n] + part(level, t, 2)
        by = 2 ** (level - (2 if level == 2 else 3))
        return p[:, :R] - shift_down(p[:, R : 2 * R], by) - shift_up(p[:, 2 * R :], by)

    prepare(3)
    for t in range(2):
        obuf[t] = finish(2, t)
        for u in range(2):
            G[0, 2 * t + u, 0] = obuf[t, pl.ds(u, Qs // 2, stride=2), :]
            send(3, 2 * t + u)

    for level in range(3, levels - 1):
        prepare(level + 1)
        for w in range(4):
            G[level - 2, w, 0] = finish(level, w)
            send(level + 1, w)

    def swapped(w):
        t, u = w // 2, w % 2
        pair_copy(2 + w, es.at[w], ex.at[w]).wait_recv()
        new, got = es[w], turn_lanes(ex[w])
        both = jnp.where(low(new) == (core == 0), new, got)
        for cz in range(nz):
            back[t, cz, :, u, :] = both[cz * NY : (cz + 1) * NY]
        if u == 1:
            home(t)

    def home(t):
        own = pltpu.make_async_copy(back.at[t, z, y], bdst.at[t, y, z], a2a_recv.at[2 + t])
        for bz in range(nz // 2, -1, -1):
            for dz in both_ways(bz) if bz else (0,):
                for dy in range(NY):
                    if dz or dy:
                        pltpu.make_async_remote_copy(
                            src_ref=back.at[t, z_of(dz), y_of(dy)], dst_ref=bdst.at[t, y, z],
                            send_sem=a2a_send.at[2 + t], recv_sem=a2a_recv.at[2 + t],
                            device_id=(z_of(dz) * NY + y_of(dy), rows), device_id_type=MESH,
                        ).start()
        own.start()

    for w in range(4):
        es[w] = finish(levels - 1, w)
        pair_copy(2 + w, es.at[w], ex.at[w]).start()
        if w:
            swapped(w - 1)
    swapped(3)

    for level in range(levels):
        for t in range(2 if level < 3 else 4):
            sent(level, t)
    for g in range(len(groups)):
        for f in range(3):
            remote_factor(g, f).wait_send()
    gone(0, src.at[:, pl.ds(0, NY - 1)])
    gone(1, ybuf.at[:, pl.ds(0, nz - 1)])
    for t in range(2):
        pair_copy(t, hs.at[t], hx.at[t]).wait_send()
    for w in range(4):
        pair_copy(2 + w, es.at[w], ex.at[w]).wait_send()
    for t in range(2):
        landed(2 + t, bdst.at[t])
        for j in range(2):
            m = 2 * j + t
            for cy in range(NY):
                turn[m, pl.ds(cy, nz, stride=NY), :] = bdst[t, cy, :, j, :]
            wide = jnp.transpose(turn[m])
            out[:, m * 2 * C : (m + 1) * 2 * C] = jnp.concatenate((wide[:dev_rows], wide[dev_rows:]), axis=1)
    for t in range(2):
        gone(2 + t, zbuf)


def solution(mesh):
    n_chain, n_rows = mesh.shape["chain"], mesh.shape["rows"]
    assert n_rows == 2 * NX and n_chain % NY == 0

    def on_device(rhs, diag, left_f, right_f):
        levels, dev_rows, M = diag.shape
        n_half = rhs.shape[1] // n_chain // 2
        C, R = n_chain, 2 * dev_rows
        nz = C // NY
        Q = C * n_half
        Qs = Q // 2
        Qh = Qs + HALO
        groups = ((0, 1), (1, 3), (3, levels))
        scratch = [
            pltpu.VMEM(rhs.shape, F32),
            pltpu.VMEM((nz, NY, n_half, R), F32),
            pltpu.VMEM((NY, nz, n_half, R), F32),
            pltpu.VMEM((nz, NY, n_half, R), F32),
            pltpu.VMEM((2, 2, NX, Qh, R), F32),
            pltpu.VMEM((2, NX, Qs, R), F32),
            pltpu.VMEM((levels - 3, 4, NX, Qs // 2, R), F32),
            pltpu.VMEM((3, levels, 2, dev_rows, M), F32),
            pltpu.VMEM((3 * R, M // 2), BF16),
            pltpu.VMEM((3 * R, M // 2), BF16),
            pltpu.VMEM((levels, 3 * R, M), BF16),
            pltpu.VMEM((levels, 3 * R, M), BF16),
            pltpu.VMEM((4, Qs, M), BF16),
            pltpu.VMEM((4, Qs, M), BF16),
            pltpu.VMEM((4, Qs, 3 * R), F32),
            pltpu.VMEM((Qh, 3 * R), F32),
            pltpu.VMEM((2, Qh, R), F32),
            pltpu.VMEM((2, Qh, R), F32),
            pltpu.VMEM((2, Qs, R), F32),
            pltpu.VMEM((4, Qs // 2, R), F32),
            pltpu.VMEM((4, Qs // 2, R), F32),
            pltpu.VMEM((2, nz, NY, 2, R), F32),
            pltpu.VMEM((C - 1, 2, R), F32),
            pltpu.VMEM((2, NY, nz, 2, R), F32),
            pltpu.VMEM((n_half, C, R), F32),
            pltpu.SemaphoreType.DMA((len(groups), 3)),
            pltpu.SemaphoreType.DMA((len(groups), 3)),
            pltpu.SemaphoreType.DMA((len(groups), 3)),
            pltpu.SemaphoreType.DMA((6,)),
            pltpu.SemaphoreType.DMA((6,)),
            pltpu.SemaphoreType.DMA((4,)),
            pltpu.SemaphoreType.DMA((4,)),
            pltpu.SemaphoreType.DMA((levels, 4)),
            pltpu.SemaphoreType.DMA((levels, 4, 3)),
            pltpu.SemaphoreType.DMA((2, 2, 3)),
            pltpu.SemaphoreType.DMA,
            pltpu.SemaphoreType.REGULAR,
        ]
        vm = pl.BlockSpec(memory_space=pltpu.VMEM)
        hbm = pl.BlockSpec(memory_space=pl.ANY)
        return pl.pallas_call(
            functools.partial(kernel, n_chain, levels, groups),
            out_shape=jax.ShapeDtypeStruct(rhs.shape, F32),
            in_specs=[hbm, hbm, hbm, hbm],
            out_specs=vm,
            scratch_shapes=scratch,
            compiler_params=pltpu.CompilerParams(
                collective_id=0, has_side_effects=True, vmem_limit_bytes=215 * 2**18
            ),
        )(rhs, diag, left_f, right_f)

    placed = (
        P("rows", "chain"),
        P(None, "rows", None),
        P(None, "rows", None),
        P(None, "rows", None),
    )
    return jax.shard_map(
        on_device, mesh=mesh, in_specs=placed, out_specs=P("rows", "chain"), check_vma=False
    )
```

```python
import functools

import jax
import jax.numpy as jnp
from jax import lax
from jax.experimental import pallas as pl
from jax.experimental.pallas import tpu as pltpu
from jax.sharding import PartitionSpec as P

MESH = pl.DeviceIdType.MESH
F32 = jnp.float32
BF16 = jnp.bfloat16
NX = 4
NY = 4
HALO = 8
ORDER = (0, 2, 1, 3)


def shift_down(v, by):
    n, w = v.shape
    if by % 8 == 0:
        return jnp.concatenate((jnp.zeros((by, w), v.dtype), v[: n - by]), axis=0)
    rows = lax.broadcasted_iota(jnp.int32, v.shape, 0)
    return jnp.where(rows < by, 0.0, pltpu.roll(v, by, 0))


def shift_up(v, by):
    n, w = v.shape
    if by % 8 == 0:
        return jnp.concatenate((v[by:], jnp.zeros((by, w), v.dtype)), axis=0)
    rows = lax.broadcasted_iota(jnp.int32, v.shape, 0)
    return jnp.where(rows >= n - by, 0.0, pltpu.roll(v, n - by, 0))


def dot_t(a, b):
    return lax.dot_general(a, b, (((1,), (1,)), ((), ())), preferred_element_type=F32)


def three_pass(v, f_hi, f_lo):
    hi = v.astype(BF16)
    lo = (v - hi.astype(F32)).astype(BF16)
    return dot_t(hi, f_hi) + dot_t(lo, f_hi) + dot_t(hi, f_lo)


def kernel(
    n_chain, levels, groups,
    rhs, diag, left_f, right_f, out,
    x2, src, ybuf, g0, GN, G2, G, fraw, f0hi, f0lo, fhi, flo, ghi, glo, prod, first_half, hs, hx, obuf, es, ex, back, zbuf, bdst, turn,
    loc_sem, fsend_sem, frecv_sem, pair_send, pair_recv, a2a_send, a2a_recv, ag_send, ag_recv, own_sem, known,
):
    C = n_chain
    nz = C // NY
    dev_rows = rhs.shape[0]
    R = 2 * dev_rows
    n_half = src.shape[2]
    Q = C * n_half
    Qs = Q // 2
    Qh = Qs + HALO
    chain = lax.axis_index("chain")
    rows = lax.axis_index("rows")
    core = lax.rem(rows, 2)
    x = rows // 2
    y = lax.rem(chain, NY)
    z = chain // NY
    partner = (chain, x * 2 + (1 - core))
    right = (chain, lax.rem(x + 1, NX) * 2 + core)
    left = (chain, lax.rem(x + NX - 1, NX) * 2 + core)
    across = (chain, lax.rem(x + 2, NX) * 2 + core)
    facs = (diag, left_f, right_f)

    def z_of(by):
        return lax.rem(z + by + nz, nz)

    def y_of(by):
        return lax.rem(y + by, NY)

    def z_dev(by):
        return (z_of(by) * NY + y, rows)

    def y_dev(by):
        return (z * NY + y_of(by), rows)

    def both_ways(by):
        return (by,) if 2 * by == nz else (by, -by)

    def signal(sem, dev):
        pl.semaphore_signal(sem, inc=1, device_id=dev, device_id_type=MESH)

    barrier = pltpu.get_barrier_semaphore()
    reach = min(4, nz // 2)
    near = [z_dev(by) for b in range(reach, 0, -1) for by in both_ways(b)]
    near += [y_dev(b) for b in range(1, NY)] + [across, right, left, partner]
    for dev in near:
        signal(barrier, dev)

    def local_factor(g, f):
        lo, hi = groups[g]
        return pltpu.make_async_copy(
            facs[f].at[lo:hi], fraw.at[f, lo:hi, core], loc_sem.at[g]
        )

    own_rhs = pltpu.make_async_copy(rhs, x2, own_sem)
    own_rhs.start()
    for g in range(len(groups)):
        for f in range(3):
            local_factor(g, f).start()

    own_rhs.wait()
    for m in range(n_half):
        turned = jnp.transpose(x2[:, m * 2 * C : (m + 1) * 2 * C])
        pairs = jnp.concatenate((turned[:C], turned[C:]), axis=1)
        for cz in range(nz):
            src[cz, :, m, :] = pairs[cz * NY : (cz + 1) * NY]

    pl.semaphore_wait(barrier, len(near))

    far = nz // 2 > reach
    if far:
        for by in both_ways(reach):
            signal(known, z_dev(by))

    def pair_copy(k, source, target):
        return pltpu.make_async_remote_copy(
            src_ref=source, dst_ref=target, send_sem=pair_send.at[0 if k < 2 else 1], recv_sem=pair_recv.at[k],
            device_id=partner, device_id_type=MESH,
        )

    def remote_factor(g, f):
        lo, hi = groups[g]
        return pltpu.make_async_remote_copy(
            src_ref=facs[f].at[lo:hi], dst_ref=fraw.at[f, lo:hi, core],
            send_sem=fsend_sem.at[g], recv_sem=frecv_sem.at[g],
            device_id=partner, device_id_type=MESH,
        )

    def phase(k, source, target, mine, others):
        own = pltpu.make_async_copy(source(mine), target.at[mine], a2a_recv.at[k])
        for place, dev in others:
            pltpu.make_async_remote_copy(
                src_ref=source(place), dst_ref=target.at[mine],
                send_sem=a2a_send.at[k], recv_sem=a2a_recv.at[k],
                device_id=dev, device_id_type=MESH,
            ).start()
        own.start()

    def landed(k, target):
        pltpu.make_async_copy(target, target, a2a_recv.at[k]).wait()

    def gone(k, part):
        pltpu.make_async_copy(part, part, a2a_send.at[k]).wait()

    y_others = [(y_of(b), y_dev(b)) for b in range(1, NY)]
    z_others = []
    for b in range(nz // 2, 0, -1):
        for by in both_ways(b):
            z_others.append((z_of(by), z_dev(by)))

    phase(0, lambda p: src.at[:, p], ybuf, y, y_others)
    for g in range(len(groups)):
        for f in range(3):
            remote_factor(g, f).start()
    landed(0, ybuf)
    if far:
        pl.semaphore_wait(known, 2)
    phase(1, lambda p: ybuf.at[:, p], g0, z, z_others)

    def factors_here(level):
        for g, (lo, _) in enumerate(groups):
            if lo == level:
                for sem, side in ((loc_sem, core), (frecv_sem, 1 - core)):
                    three = fraw.at[:, lo : groups[g][1], side]
                    pltpu.make_async_copy(three, three, sem.at[g]).wait()

    def columns(f, level, slot):
        at = pl.multiple_of(lax.rem(x + NX - ORDER[slot], NX) * R, R)
        return fraw[f, level, :, :, pl.ds(at, R)].reshape(R, R)

    def prepare(level):
        factors_here(level)
        for f in range(3):
            for rel in range(NX):
                v = columns(f, level, rel)
                hi = v.astype(BF16)
                fhi[level, f * R : (f + 1) * R, rel * R : (rel + 1) * R] = hi
                flo[level, f * R : (f + 1) * R, rel * R : (rel + 1) * R] = (v - hi.astype(F32)).astype(BF16)

    def low(v):
        return lax.broadcasted_iota(jnp.int32, v.shape, 1) < dev_rows

    def turn_lanes(v):
        return pltpu.roll(v, dev_rows, 1)

    def firsts(a, b):
        return jnp.where(low(a), a, turn_lanes(b))

    def seconds(a, b):
        return jnp.where(low(a), turn_lanes(a), b)

    def prepare_first():
        factors_here(0)
        for f in range(3):
            for k in range(NX // 2):
                a, b = columns(f, 0, 2 * k), columns(f, 0, 2 * k + 1)
                v = jnp.where(core == 0, firsts(a, b), seconds(a, b))
                hi = v.astype(BF16)
                f0hi[f * R : (f + 1) * R, k * R : (k + 1) * R] = hi
                f0lo[f * R : (f + 1) * R, k * R : (k + 1) * R] = (v - hi.astype(F32)).astype(BF16)

    route = ((1, across), (2, right), (3, left))

    def chunk(level, t, slot):
        if level < 2:
            return GN.at[level, t, slot]
        return G2.at[t, slot] if level == 2 else G.at[level - 3, t, slot]

    def hop(level, t, k, piece=None):
        slot, dev = route[k]
        source, target, recv = chunk(level, t, 0), chunk(level, t, slot), ag_recv.at[level % 2, t, k]
        if piece is not None:
            some = pl.ds(piece * (Qs // 2), Qs // 2)
            source, target, recv = source.at[some], target.at[some], ag_recv.at[0, 2 * t + piece, k]
        return pltpu.make_async_remote_copy(
            src_ref=source, dst_ref=target, send_sem=ag_send.at[level % 2, t], recv_sem=recv,
            device_id=dev, device_id_type=MESH,
        )

    def send(level, t, piece=None):
        if level >= 2 and piece != 1:
            if level >= 5 or t < 2:
                sent(level - 2, t)
        for k in range(3):
            hop(level, t, k, piece).start()

    def arrived(level, t, k):
        if level == 2:
            for piece in range(2):
                hop(level, t, k, piece).wait_recv()
        else:
            hop(level, t, k).wait_recv()

    def sent(level, t):
        part = chunk(level, t, pl.ds(0, 3))
        pltpu.make_async_copy(part, part, ag_send.at[level % 2, t]).wait()

    def padded(v):
        return jnp.concatenate((v, jnp.zeros((HALO, v.shape[1]), F32)), axis=0)

    prepare_first()
    landed(1, g0)
    first = (0, (Qs - HALO) // n_half)
    for t in range(2):
        for i in range(Qh // n_half):
            c = first[t] + i
            GN[0, t, 0, i * n_half : (i + 1) * n_half, :] = g0[c // NY, c % NY]
        send(0, t)
    prepare(1)
    for t in range(2):
        for k in (1, 2, 0):
            arrived(0, t, k)
        a = [GN[0, t, rel] for rel in range(NX)]
        ev = jnp.concatenate((firsts(a[0], a[1]), firsts(a[2], a[3])), axis=1)
        pe = three_pass(padded(ev), f0hi[...], f0lo[...])[:Qh]
        od = jnp.concatenate((seconds(a[0], a[1]), seconds(a[2], a[3])), axis=1)
        po = three_pass(padded(od), f0hi[...], f0lo[...])[:Qh]
        to_even = pe[:, :R] - shift_down(po[:, R : 2 * R], 1) - po[:, 2 * R :]
        to_odd = po[:, :R] - pe[:, R : 2 * R] - shift_up(pe[:, 2 * R :], 1)
        hs[t] = jnp.where(core == 0, to_odd, to_even)
        other = pair_copy(t, hs.at[t], hx.at[t])
        other.start()
        mine = jnp.where(core == 0, to_even, to_odd)
        other.wait_recv()
        GN[1, t, 0] = mine + hx[t]
        send(1, t)

    prepare(2)
    for t in range(2):
        arrived(1, t, 0)
        v = padded(jnp.concatenate((GN[1, t, 0], GN[1, t, 1]), axis=1))
        first_half[...] = three_pass(v, fhi[1, :, : 2 * R], flo[1, :, : 2 * R])[:Qh]
        arrived(1, t, 1)
        arrived(1, t, 2)
        v = padded(jnp.concatenate((GN[1, t, 2], GN[1, t, 3]), axis=1))
        p = first_half[...] + three_pass(v, fhi[1, :, 2 * R :], flo[1, :, 2 * R :])[:Qh]
        new = p[:, :R] - shift_down(p[:, R : 2 * R], 1) - shift_up(p[:, 2 * R :], 1)
        obuf[t] = new[:Qs] if t == 0 else new[HALO:]
        for u in range(2):
            G2[u, 0, t * (Qs // 2) : (t + 1) * (Qs // 2), :] = obuf[t, pl.ds(u, Qs // 2, stride=2), :]
            send(2, u, t)

    def part(level, t, first):
        n = Qs if level == 2 else Qs // 2
        for slot in (first, first + 1):
            v = chunk(level, t, slot)[...]
            hi = v.astype(BF16)
            ghi[t, :n, slot * R : (slot + 1) * R] = hi
            glo[t, :n, slot * R : (slot + 1) * R] = (v - hi.astype(F32)).astype(BF16)
        ks = slice(first * R, (first + 2) * R)
        a, b = ghi[t, :n, ks], fhi[level, :, ks]
        return dot_t(a, b) + dot_t(glo[t, :n, ks], b) + dot_t(a, flo[level, :, ks])

    def finish(level, t):
        n = Qs if level == 2 else Qs // 2
        arrived(level, t, 0)
        prod[t, :n] = part(level, t, 0)
        arrived(level, t, 1)
        arrived(level, t, 2)
        p = prod[t, :n] + part(level, t, 2)
        by = 2 ** (level - (2 if level == 2 else 3))
        return p[:, :R] - shift_down(p[:, R : 2 * R], by) - shift_up(p[:, 2 * R :], by)

    prepare(3)
    for t in range(2):
        obuf[t] = finish(2, t)
        for u in range(2):
            G[0, 2 * t + u, 0] = obuf[t, pl.ds(u, Qs // 2, stride=2), :]
            send(3, 2 * t + u)

    for level in range(3, levels - 1):
        prepare(level + 1)
        for w in range(4):
            G[level - 2, w, 0] = finish(level, w)
            send(level + 1, w)

    def swapped(w):
        pair_copy(2 + w, es.at[w], ex.at[w]).wait_recv()
        new, got = es[w], turn_lanes(ex[w])
        both = jnp.where(low(new) == (core == 0), new, got)
        for cz in range(nz):
            back[w, cz, :, 0, :] = both[cz * NY : (cz + 1) * NY]
        home(w)

    def home(t):
        own = pltpu.make_async_copy(back.at[t, z, y], bdst.at[t, y, z], a2a_recv.at[2 + t])
        for bz in range(nz // 2, -1, -1):
            for dz in both_ways(bz) if bz else (0,):
                for dy in range(NY):
                    if dz or dy:
                        pltpu.make_async_remote_copy(
                            src_ref=back.at[t, z_of(dz), y_of(dy)], dst_ref=bdst.at[t, y, z],
                            send_sem=a2a_send.at[2], recv_sem=a2a_recv.at[2 + t],
                            device_id=(z_of(dz) * NY + y_of(dy), rows), device_id_type=MESH,
                        ).start()
        own.start()

    for w in range(4):
        es[w] = finish(levels - 1, w)
        pair_copy(2 + w, es.at[w], ex.at[w]).start()
        if w:
            swapped(w - 1)
    swapped(3)

    for level in (levels - 2, levels - 1):
        for t in range(4):
            sent(level, t)
    for g, (lo, hi) in enumerate(groups):
        three = fraw.at[:, lo:hi, core]
        pltpu.make_async_copy(three, three, fsend_sem.at[g]).wait()
    gone(0, src.at[:, pl.ds(0, NY - 1)])
    gone(1, ybuf.at[:, pl.ds(0, nz - 1)])
    for k, both in enumerate((hs, es)):
        pltpu.make_async_copy(both, both, pair_send.at[k]).wait()
    for w in range(4):
        landed(2 + w, bdst.at[w])
        m = 2 * (w % 2) + w // 2
        for cy in range(NY):
            turn[m, pl.ds(cy, nz, stride=NY), :] = bdst[w, cy, :, 0, :]
        wide = jnp.transpose(turn[m])
        out[:, m * 2 * C : (m + 1) * 2 * C] = jnp.concatenate((wide[:dev_rows], wide[dev_rows:]), axis=1)
    gone(2, zbuf)


def solution(mesh):
    n_chain, n_rows = mesh.shape["chain"], mesh.shape["rows"]
    assert n_rows == 2 * NX and n_chain % NY == 0

    def on_device(rhs, diag, left_f, right_f):
        levels, dev_rows, M = diag.shape
        n_half = rhs.shape[1] // n_chain // 2
        C, R = n_chain, 2 * dev_rows
        nz = C // NY
        Q = C * n_half
        Qs = Q // 2
        Qh = Qs + HALO
        groups = ((0, 1), (1, 3), (3, levels))
        scratch = [
            pltpu.VMEM(rhs.shape, F32),
            pltpu.VMEM((nz, NY, n_half, R), F32),
            pltpu.VMEM((NY, nz, n_half, R), F32),
            pltpu.VMEM((nz, NY, n_half, R), F32),
            pltpu.VMEM((2, 2, NX, Qh, R), F32),
            pltpu.VMEM((2, NX, Qs, R), F32),
            pltpu.VMEM((levels - 3, 4, NX, Qs // 2, R), F32),
            pltpu.VMEM((3, levels, 2, dev_rows, M), F32),
            pltpu.VMEM((3 * R, M // 2), BF16),
            pltpu.VMEM((3 * R, M // 2), BF16),
            pltpu.VMEM((levels, 3 * R, M), BF16),
            pltpu.VMEM((levels, 3 * R, M), BF16),
            pltpu.VMEM((4, Qs, M), BF16),
            pltpu.VMEM((4, Qs, M), BF16),
            pltpu.VMEM((4, Qs, 3 * R), F32),
            pltpu.VMEM((Qh, 3 * R), F32),
            pltpu.VMEM((2, Qh, R), F32),
            pltpu.VMEM((2, Qh, R), F32),
            pltpu.VMEM((2, Qs, R), F32),
            pltpu.VMEM((4, Qs // 2, R), F32),
            pltpu.VMEM((4, Qs // 2, R), F32),
            pltpu.VMEM((4, nz, NY, 1, R), F32),
            pltpu.VMEM((4, C - 1, 1, R), F32),
            pltpu.VMEM((4, NY, nz, 1, R), F32),
            pltpu.VMEM((n_half, C, R), F32),
            pltpu.SemaphoreType.DMA((len(groups),)),
            pltpu.SemaphoreType.DMA((len(groups),)),
            pltpu.SemaphoreType.DMA((len(groups),)),
            pltpu.SemaphoreType.DMA((2,)),
            pltpu.SemaphoreType.DMA((6,)),
            pltpu.SemaphoreType.DMA((3,)),
            pltpu.SemaphoreType.DMA((6,)),
            pltpu.SemaphoreType.DMA((2, 4)),
            pltpu.SemaphoreType.DMA((2, 4, 3)),
            pltpu.SemaphoreType.DMA,
            pltpu.SemaphoreType.REGULAR,
        ]
        vm = pl.BlockSpec(memory_space=pltpu.VMEM)
        hbm = pl.BlockSpec(memory_space=pl.ANY)
        return pl.pallas_call(
            functools.partial(kernel, n_chain, levels, groups),
            out_shape=jax.ShapeDtypeStruct(rhs.shape, F32),
            in_specs=[hbm, hbm, hbm, hbm],
            out_specs=vm,
            scratch_shapes=scratch,
            compiler_params=pltpu.CompilerParams(
                collective_id=0, has_side_effects=True, vmem_limit_bytes=215 * 2**18
            ),
        )(rhs, diag, left_f, right_f)

    placed = (
        P("rows", "chain"),
        P(None, "rows", None),
        P(None, "rows", None),
        P(None, "rows", None),
    )
    return jax.shard_map(
        on_device, mesh=mesh, in_specs=placed, out_specs=P("rows", "chain"), check_vma=False
    )
```

```python
import functools

import jax
import jax.numpy as jnp
from jax import lax
from jax.experimental import pallas as pl
from jax.experimental.pallas import tpu as pltpu
from jax.sharding import PartitionSpec as P

MESH = pl.DeviceIdType.MESH
F32 = jnp.float32
BF16 = jnp.bfloat16
NX = 4
NY = 4
HALO = 8
ORDER = (0, 2, 1, 3)


def shift_down(v, by):
    n, w = v.shape
    if by % 8 == 0:
        return jnp.concatenate((jnp.zeros((by, w), v.dtype), v[: n - by]), axis=0)
    rows = lax.broadcasted_iota(jnp.int32, v.shape, 0)
    return jnp.where(rows < by, 0.0, pltpu.roll(v, by, 0))


def shift_up(v, by):
    n, w = v.shape
    if by % 8 == 0:
        return jnp.concatenate((v[by:], jnp.zeros((by, w), v.dtype)), axis=0)
    rows = lax.broadcasted_iota(jnp.int32, v.shape, 0)
    return jnp.where(rows >= n - by, 0.0, pltpu.roll(v, n - by, 0))


def dot_t(a, b):
    return lax.dot_general(a, b, (((1,), (1,)), ((), ())), preferred_element_type=F32)


def three_pass(v, f_hi, f_lo):
    hi = v.astype(BF16)
    lo = (v - hi.astype(F32)).astype(BF16)
    n = v.shape[0]
    p = dot_t(jnp.concatenate((hi, lo), axis=0), f_hi)
    return p[:n] + p[n:] + dot_t(hi, f_lo)


def kernel(
    n_chain, levels, groups,
    rhs, diag, left_f, right_f, out,
    x2, src, ybuf, g0, GN, G2, G, fraw, f0hi, f0lo, fhi, flo, both, prod, first_half, hs, hx, obuf, es, ex, back, zbuf, bdst, turn,
    loc_sem, fsend_sem, frecv_sem, pair_send, pair_recv, a2a_send, a2a_recv, ag_send, ag_recv, own_sem, known,
):
    C = n_chain
    nz = C // NY
    dev_rows = rhs.shape[0]
    R = 2 * dev_rows
    n_half = src.shape[2]
    Q = C * n_half
    Qs = Q // 2
    Qh = Qs + HALO
    chain = lax.axis_index("chain")
    rows = lax.axis_index("rows")
    core = lax.rem(rows, 2)
    x = rows // 2
    y = lax.rem(chain, NY)
    z = chain // NY
    partner = (chain, x * 2 + (1 - core))
    right = (chain, lax.rem(x + 1, NX) * 2 + core)
    left = (chain, lax.rem(x + NX - 1, NX) * 2 + core)
    across = (chain, lax.rem(x + 2, NX) * 2 + core)
    facs = (diag, left_f, right_f)

    def z_of(by):
        return lax.rem(z + by + nz, nz)

    def y_of(by):
        return lax.rem(y + by, NY)

    def z_dev(by):
        return (z_of(by) * NY + y, rows)

    def y_dev(by):
        return (z * NY + y_of(by), rows)

    def both_ways(by):
        return (by,) if 2 * by == nz else (by, -by)

    def signal(sem, dev):
        pl.semaphore_signal(sem, inc=1, device_id=dev, device_id_type=MESH)

    barrier = pltpu.get_barrier_semaphore()
    reach = min(4, nz // 2)
    near = [z_dev(by) for b in range(reach, 0, -1) for by in both_ways(b)]
    near += [y_dev(b) for b in range(1, NY)] + [across, right, left, partner]
    for dev in near:
        signal(barrier, dev)

    def local_factor(g, f):
        lo, hi = groups[g]
        return pltpu.make_async_copy(
            facs[f].at[lo:hi], fraw.at[f, lo:hi, core], loc_sem.at[g]
        )

    own_rhs = pltpu.make_async_copy(rhs, x2, own_sem)
    own_rhs.start()
    for g in range(len(groups)):
        for f in range(3):
            local_factor(g, f).start()

    own_rhs.wait()
    for m in range(n_half):
        turned = jnp.transpose(x2[:, m * 2 * C : (m + 1) * 2 * C])
        pairs = jnp.concatenate((turned[:C], turned[C:]), axis=1)
        for cz in range(nz):
            src[cz, :, m, :] = pairs[cz * NY : (cz + 1) * NY]

    pl.semaphore_wait(barrier, len(near))

    far = nz // 2 > reach
    if far:
        for by in both_ways(reach):
            signal(known, z_dev(by))

    def pair_copy(k, source, target):
        return pltpu.make_async_remote_copy(
            src_ref=source, dst_ref=target, send_sem=pair_send.at[0 if k < 2 else 1], recv_sem=pair_recv.at[k],
            device_id=partner, device_id_type=MESH,
        )

    def remote_factor(g, f):
        lo, hi = groups[g]
        return pltpu.make_async_remote_copy(
            src_ref=facs[f].at[lo:hi], dst_ref=fraw.at[f, lo:hi, core],
            send_sem=fsend_sem.at[g], recv_sem=frecv_sem.at[g],
            device_id=partner, device_id_type=MESH,
        )

    def phase(k, source, target, mine, others):
        own = pltpu.make_async_copy(source(mine), target.at[mine], a2a_recv.at[k])
        for place, dev in others:
            pltpu.make_async_remote_copy(
                src_ref=source(place), dst_ref=target.at[mine],
                send_sem=a2a_send.at[k], recv_sem=a2a_recv.at[k],
                device_id=dev, device_id_type=MESH,
            ).start()
        own.start()

    def landed(k, target):
        pltpu.make_async_copy(target, target, a2a_recv.at[k]).wait()

    def gone(k, part):
        pltpu.make_async_copy(part, part, a2a_send.at[k]).wait()

    y_others = [(y_of(b), y_dev(b)) for b in range(1, NY)]
    z_others = []
    for b in range(nz // 2, 0, -1):
        for by in both_ways(b):
            z_others.append((z_of(by), z_dev(by)))

    phase(0, lambda p: src.at[:, p], ybuf, y, y_others)
    for g in range(len(groups)):
        for f in range(3):
            remote_factor(g, f).start()
    landed(0, ybuf)
    if far:
        pl.semaphore_wait(known, 2)
    phase(1, lambda p: ybuf.at[:, p], g0, z, z_others)

    def factors_here(level):
        for g, (lo, _) in enumerate(groups):
            if lo == level:
                for sem, side in ((loc_sem, core), (frecv_sem, 1 - core)):
                    three = fraw.at[:, lo : groups[g][1], side]
                    pltpu.make_async_copy(three, three, sem.at[g]).wait()

    def columns(f, level, slot):
        at = pl.multiple_of(lax.rem(x + NX - ORDER[slot], NX) * R, R)
        return fraw[f, level, :, :, pl.ds(at, R)].reshape(R, R)

    def prepare(level):
        factors_here(level)
        for f in range(3):
            for rel in range(NX):
                v = columns(f, level, rel)
                hi = v.astype(BF16)
                fhi[level, f * R : (f + 1) * R, rel * R : (rel + 1) * R] = hi
                flo[level, f * R : (f + 1) * R, rel * R : (rel + 1) * R] = (v - hi.astype(F32)).astype(BF16)

    def low(v):
        return lax.broadcasted_iota(jnp.int32, v.shape, 1) < dev_rows

    def turn_lanes(v):
        return pltpu.roll(v, dev_rows, 1)

    def firsts(a, b):
        return jnp.where(low(a), a, turn_lanes(b))

    def seconds(a, b):
        return jnp.where(low(a), turn_lanes(a), b)

    def prepare_first():
        factors_here(0)
        for f in range(3):
            for k in range(NX // 2):
                a, b = columns(f, 0, 2 * k), columns(f, 0, 2 * k + 1)
                v = jnp.where(core == 0, firsts(a, b), seconds(a, b))
                hi = v.astype(BF16)
                f0hi[f * R : (f + 1) * R, k * R : (k + 1) * R] = hi
                f0lo[f * R : (f + 1) * R, k * R : (k + 1) * R] = (v - hi.astype(F32)).astype(BF16)

    route = ((1, across), (2, right), (3, left))

    def chunk(level, t, slot):
        if level < 2:
            return GN.at[level, t, slot]
        return G2.at[t, slot] if level == 2 else G.at[level - 3, t, slot]

    def hop(level, t, k, piece=None):
        slot, dev = route[k]
        source, target, recv = chunk(level, t, 0), chunk(level, t, slot), ag_recv.at[level % 2, t, k]
        if piece is not None:
            some = pl.ds(piece * (Qs // 2), Qs // 2)
            source, target, recv = source.at[some], target.at[some], ag_recv.at[0, 2 * t + piece, k]
        return pltpu.make_async_remote_copy(
            src_ref=source, dst_ref=target, send_sem=ag_send.at[level % 2, t], recv_sem=recv,
            device_id=dev, device_id_type=MESH,
        )

    def send(level, t, piece=None):
        if level >= 2 and piece != 1:
            if level >= 5 or t < 2:
                sent(level - 2, t)
        for k in range(3):
            hop(level, t, k, piece).start()

    def arrived(level, t, k):
        if level == 2:
            for piece in range(2):
                hop(level, t, k, piece).wait_recv()
        else:
            hop(level, t, k).wait_recv()

    def sent(level, t):
        part = chunk(level, t, pl.ds(0, 3))
        pltpu.make_async_copy(part, part, ag_send.at[level % 2, t]).wait()

    def padded(v):
        return jnp.concatenate((v, jnp.zeros((HALO, v.shape[1]), F32)), axis=0)

    prepare_first()
    landed(1, g0)
    first = (0, (Qs - HALO) // n_half)
    for t in range(2):
        for i in range(Qh // n_half):
            c = first[t] + i
            GN[0, t, 0, i * n_half : (i + 1) * n_half, :] = g0[c // NY, c % NY]
        send(0, t)
    prepare(1)
    for t in range(2):
        for k in (1, 2, 0):
            arrived(0, t, k)
        a = [GN[0, t, rel] for rel in range(NX)]
        ev = jnp.concatenate((firsts(a[0], a[1]), firsts(a[2], a[3])), axis=1)
        pe = three_pass(padded(ev), f0hi[...], f0lo[...])[:Qh]
        od = jnp.concatenate((seconds(a[0], a[1]), seconds(a[2], a[3])), axis=1)
        po = three_pass(padded(od), f0hi[...], f0lo[...])[:Qh]
        to_even = pe[:, :R] - shift_down(po[:, R : 2 * R], 1) - po[:, 2 * R :]
        to_odd = po[:, :R] - pe[:, R : 2 * R] - shift_up(pe[:, 2 * R :], 1)
        hs[t] = jnp.where(core == 0, to_odd, to_even)
        other = pair_copy(t, hs.at[t], hx.at[t])
        other.start()
        mine = jnp.where(core == 0, to_even, to_odd)
        other.wait_recv()
        GN[1, t, 0] = mine + hx[t]
        send(1, t)

    prepare(2)
    for t in range(2):
        arrived(1, t, 0)
        v = padded(jnp.concatenate((GN[1, t, 0], GN[1, t, 1]), axis=1))
        first_half[...] = three_pass(v, fhi[1, :, : 2 * R], flo[1, :, : 2 * R])[:Qh]
        arrived(1, t, 1)
        arrived(1, t, 2)
        v = padded(jnp.concatenate((GN[1, t, 2], GN[1, t, 3]), axis=1))
        p = first_half[...] + three_pass(v, fhi[1, :, 2 * R :], flo[1, :, 2 * R :])[:Qh]
        new = p[:, :R] - shift_down(p[:, R : 2 * R], 1) - shift_up(p[:, 2 * R :], 1)
        obuf[t] = new[:Qs] if t == 0 else new[HALO:]
        for u in range(2):
            G2[u, 0, t * (Qs // 2) : (t + 1) * (Qs // 2), :] = obuf[t, pl.ds(u, Qs // 2, stride=2), :]
            send(2, u, t)

    def part(level, t, first):
        n, base = (Qs, 4) if level == 2 else (Qs // 2, 0)
        for slot in (first, first + 1):
            if slot == 0 and level > 2:
                continue
            v = chunk(level, t, slot)[...]
            hi = v.astype(BF16)
            both[t + base, :n, slot * R : (slot + 1) * R] = hi
            both[t + base, n : 2 * n, slot * R : (slot + 1) * R] = (v - hi.astype(F32)).astype(BF16)
        ks = slice(first * R, (first + 2) * R)
        p = dot_t(both[t + base, : 2 * n, ks], fhi[level, :, ks])
        return p[:n] + p[n:] + dot_t(both[t + base, :n, ks], flo[level, :, ks])

    def finish(level, t):
        n = Qs if level == 2 else Qs // 2
        arrived(level, t, 0)
        prod[t, :n] = part(level, t, 0)
        arrived(level, t, 1)
        arrived(level, t, 2)
        p = prod[t, :n] + part(level, t, 2)
        by = 2 ** (level - (2 if level == 2 else 3))
        return p[:, :R] - shift_down(p[:, R : 2 * R], by) - shift_up(p[:, 2 * R :], by)

    def own_chunk(level, w, v):
        G[level - 3, w, 0] = v
        send(level, w)
        hi = v.astype(BF16)
        both[w, : Qs // 2, :R] = hi
        both[w, Qs // 2 : Qs, :R] = (v - hi.astype(F32)).astype(BF16)

    prepare(3)
    for t in range(2):
        obuf[t] = finish(2, t)
        for u in range(2):
            own_chunk(3, 2 * t + u, obuf[t, pl.ds(u, Qs // 2, stride=2), :])

    for level in range(3, levels - 1):
        prepare(level + 1)
        for w in range(4):
            own_chunk(level + 1, w, finish(level, w))

    def swapped(w):
        pair_copy(2 + w, es.at[w], ex.at[w]).wait_recv()
        new, got = es[w], turn_lanes(ex[w])
        packed = jnp.where(low(new) == (core == 0), new, got)
        for cz in range(nz):
            back[w, cz, :, 0, :] = packed[cz * NY : (cz + 1) * NY]
        home(w)

    def home(t):
        own = pltpu.make_async_copy(back.at[t, z, y], bdst.at[t, y, z], a2a_recv.at[2 + t])
        for bz in range(nz // 2, -1, -1):
            for dz in both_ways(bz) if bz else (0,):
                for dy in range(NY):
                    if dz or dy:
                        pltpu.make_async_remote_copy(
                            src_ref=back.at[t, z_of(dz), y_of(dy)], dst_ref=bdst.at[t, y, z],
                            send_sem=a2a_send.at[2], recv_sem=a2a_recv.at[2 + t],
                            device_id=(z_of(dz) * NY + y_of(dy), rows), device_id_type=MESH,
                        ).start()
        own.start()

    for w in range(4):
        es[w] = finish(levels - 1, w)
        pair_copy(2 + w, es.at[w], ex.at[w]).start()
        if w:
            swapped(w - 1)
    swapped(3)

    for level in (levels - 2, levels - 1):
        for t in range(4):
            sent(level, t)
    for g, (lo, hi) in enumerate(groups):
        three = fraw.at[:, lo:hi, core]
        pltpu.make_async_copy(three, three, fsend_sem.at[g]).wait()
    gone(0, src.at[:, pl.ds(0, NY - 1)])
    gone(1, ybuf.at[:, pl.ds(0, nz - 1)])
    for k, source in enumerate((hs, es)):
        pltpu.make_async_copy(source, source, pair_send.at[k]).wait()
    for w in range(4):
        landed(2 + w, bdst.at[w])
        m = 2 * (w % 2) + w // 2
        for cy in range(NY):
            turn[m, pl.ds(cy, nz, stride=NY), :] = bdst[w, cy, :, 0, :]
        wide = jnp.transpose(turn[m])
        out[:, m * 2 * C : (m + 1) * 2 * C] = jnp.concatenate((wide[:dev_rows], wide[dev_rows:]), axis=1)
    gone(2, zbuf)


def solution(mesh):
    n_chain, n_rows = mesh.shape["chain"], mesh.shape["rows"]
    assert n_rows == 2 * NX and n_chain % NY == 0

    def on_device(rhs, diag, left_f, right_f):
        levels, dev_rows, M = diag.shape
        n_half = rhs.shape[1] // n_chain // 2
        C, R = n_chain, 2 * dev_rows
        nz = C // NY
        Q = C * n_half
        Qs = Q // 2
        Qh = Qs + HALO
        groups = ((0, 1), (1, 3), (3, levels))
        scratch = [
            pltpu.VMEM(rhs.shape, F32),
            pltpu.VMEM((nz, NY, n_half, R), F32),
            pltpu.VMEM((NY, nz, n_half, R), F32),
            pltpu.VMEM((nz, NY, n_half, R), F32),
            pltpu.VMEM((2, 2, NX, Qh, R), F32),
            pltpu.VMEM((2, NX, Qs, R), F32),
            pltpu.VMEM((levels - 3, 4, NX, Qs // 2, R), F32),
            pltpu.VMEM((3, levels, 2, dev_rows, M), F32),
            pltpu.VMEM((3 * R, M // 2), BF16),
            pltpu.VMEM((3 * R, M // 2), BF16),
            pltpu.VMEM((levels, 3 * R, M), BF16),
            pltpu.VMEM((levels, 3 * R, M), BF16),
            pltpu.VMEM((6, 2 * Qs, M), BF16),
            pltpu.VMEM((4, Qs, 3 * R), F32),
            pltpu.VMEM((Qh, 3 * R), F32),
            pltpu.VMEM((2, Qh, R), F32),
            pltpu.VMEM((2, Qh, R), F32),
            pltpu.VMEM((2, Qs, R), F32),
            pltpu.VMEM((4, Qs // 2, R), F32),
            pltpu.VMEM((4, Qs // 2, R), F32),
            pltpu.VMEM((4, nz, NY, 1, R), F32),
            pltpu.VMEM((4, C - 1, 1, R), F32),
            pltpu.VMEM((4, NY, nz, 1, R), F32),
            pltpu.VMEM((n_half, C, R), F32),
            pltpu.SemaphoreType.DMA((len(groups),)),
            pltpu.SemaphoreType.DMA((len(groups),)),
            pltpu.SemaphoreType.DMA((len(groups),)),
            pltpu.SemaphoreType.DMA((2,)),
            pltpu.SemaphoreType.DMA((6,)),
            pltpu.SemaphoreType.DMA((3,)),
            pltpu.SemaphoreType.DMA((6,)),
            pltpu.SemaphoreType.DMA((2, 4)),
            pltpu.SemaphoreType.DMA((2, 4, 3)),
            pltpu.SemaphoreType.DMA,
            pltpu.SemaphoreType.REGULAR,
        ]
        vm = pl.BlockSpec(memory_space=pltpu.VMEM)
        hbm = pl.BlockSpec(memory_space=pl.ANY)
        return pl.pallas_call(
            functools.partial(kernel, n_chain, levels, groups),
            out_shape=jax.ShapeDtypeStruct(rhs.shape, F32),
            in_specs=[hbm, hbm, hbm, hbm],
            out_specs=vm,
            scratch_shapes=scratch,
            compiler_params=pltpu.CompilerParams(
                collective_id=0, has_side_effects=True, vmem_limit_bytes=215 * 2**18
            ),
        )(rhs, diag, left_f, right_f)

    placed = (
        P("rows", "chain"),
        P(None, "rows", None),
        P(None, "rows", None),
        P(None, "rows", None),
    )
    return jax.shard_map(
        on_device, mesh=mesh, in_specs=placed, out_specs=P("rows", "chain"), check_vma=False
    )
```

```python
import functools

import jax
import jax.numpy as jnp
from jax import lax
from jax.experimental import pallas as pl
from jax.experimental.pallas import tpu as pltpu
from jax.sharding import PartitionSpec as P

MESH = pl.DeviceIdType.MESH
F32 = jnp.float32
BF16 = jnp.bfloat16
NX = 4
NY = 4
HALO = 8
ORDER = (0, 2, 1, 3)


def dot_t(a, b):
    return lax.dot_general(a, b, (((1,), (1,)), ((), ())), preferred_element_type=F32)


def three_pass(v, f_hi, f_lo):
    hi = v.astype(BF16)
    lo = (v - hi.astype(F32)).astype(BF16)
    n = v.shape[0]
    p = dot_t(jnp.concatenate((hi, lo), axis=0), f_hi)
    return p[:n] + p[n:] + dot_t(hi, f_lo)


def kernel(
    n_chain, levels, groups,
    rhs, diag, left_f, right_f, out,
    x2, src, ybuf, g0, GN, G2, G, fraw, f0hi, f0lo, fhi, flo, both, prod, first_half, hs, hx, obuf, es, ex, back, zbuf, bdst, turn,
    loc_sem, fsend_sem, frecv_sem, pair_send, pair_recv, a2a_send, a2a_recv, ag_send, ag_recv, own_sem, known,
):
    C = n_chain
    nz = C // NY
    dev_rows = rhs.shape[0]
    R = 2 * dev_rows
    n_half = src.shape[2]
    Q = C * n_half
    Qs = Q // 2
    Qh = Qs + 2 * HALO
    chain = lax.axis_index("chain")
    rows = lax.axis_index("rows")
    core = lax.rem(rows, 2)
    x = rows // 2
    y = lax.rem(chain, NY)
    z = chain // NY
    partner = (chain, x * 2 + (1 - core))
    right = (chain, lax.rem(x + 1, NX) * 2 + core)
    left = (chain, lax.rem(x + NX - 1, NX) * 2 + core)
    across = (chain, lax.rem(x + 2, NX) * 2 + core)
    facs = (diag, left_f, right_f)

    def z_of(by):
        return lax.rem(z + by + nz, nz)

    def y_of(by):
        return lax.rem(y + by, NY)

    def z_dev(by):
        return (z_of(by) * NY + y, rows)

    def y_dev(by):
        return (z * NY + y_of(by), rows)

    def both_ways(by):
        return (by,) if 2 * by == nz else (by, -by)

    def signal(sem, dev):
        pl.semaphore_signal(sem, inc=1, device_id=dev, device_id_type=MESH)

    barrier = pltpu.get_barrier_semaphore()
    reach = min(4, nz // 2)
    near = [z_dev(by) for b in range(reach, 0, -1) for by in both_ways(b)]
    near += [y_dev(b) for b in range(1, NY)] + [across, right, left, partner]
    for dev in near:
        signal(barrier, dev)

    def local_factor(g, f):
        lo, hi = groups[g]
        return pltpu.make_async_copy(
            facs[f].at[lo:hi], fraw.at[f, lo:hi, core], loc_sem.at[g]
        )

    own_rhs = pltpu.make_async_copy(rhs, x2, own_sem)
    own_rhs.start()
    for g in range(len(groups)):
        for f in range(3):
            local_factor(g, f).start()

    own_rhs.wait()
    for m in range(n_half):
        turned = jnp.transpose(x2[:, m * 2 * C : (m + 1) * 2 * C])
        pairs = jnp.concatenate((turned[:C], turned[C:]), axis=1)
        for cz in range(nz):
            src[cz, :, m, :] = pairs[cz * NY : (cz + 1) * NY]

    pl.semaphore_wait(barrier, len(near))

    far = nz // 2 > reach
    if far:
        for by in both_ways(reach):
            signal(known, z_dev(by))

    def pair_copy(k, source, target):
        return pltpu.make_async_remote_copy(
            src_ref=source, dst_ref=target, send_sem=pair_send.at[0 if k < 2 else 1], recv_sem=pair_recv.at[k],
            device_id=partner, device_id_type=MESH,
        )

    def remote_factor(g, f):
        lo, hi = groups[g]
        return pltpu.make_async_remote_copy(
            src_ref=facs[f].at[lo:hi], dst_ref=fraw.at[f, lo:hi, core],
            send_sem=fsend_sem.at[g], recv_sem=frecv_sem.at[g],
            device_id=partner, device_id_type=MESH,
        )

    def phase(k, source, target, mine, others):
        own = pltpu.make_async_copy(source(mine), target.at[mine], a2a_recv.at[k])
        for place, dev in others:
            pltpu.make_async_remote_copy(
                src_ref=source(place), dst_ref=target.at[mine],
                send_sem=a2a_send.at[k], recv_sem=a2a_recv.at[k],
                device_id=dev, device_id_type=MESH,
            ).start()
        own.start()

    def landed(k, target):
        pltpu.make_async_copy(target, target, a2a_recv.at[k]).wait()

    def gone(k, part):
        pltpu.make_async_copy(part, part, a2a_send.at[k]).wait()

    y_others = [(y_of(b), y_dev(b)) for b in range(1, NY)]

    phase(0, lambda p: src.at[:, p], ybuf, y, y_others)
    for g in range(len(groups)):
        for f in range(3):
            remote_factor(g, f).start()
    landed(0, ybuf)
    if far:
        pl.semaphore_wait(known, 2)
    zsh = nz // 4
    near_n = min(nz, nz // 2 + 2)
    offset = lax.rem(z - zsh + nz, nz) * (NY * n_half)

    def slot_of(by):
        return (zsh + 1 - by) % nz

    def part_of(by):
        return 1 if slot_of(by) < near_n else 2

    here = pltpu.make_async_copy(ybuf.at[:, z], g0.at[slot_of(0)], a2a_recv.at[1])
    for by in sorted((b for n in range(1, nz // 2 + 1) for b in both_ways(n)), key=part_of):
        pltpu.make_async_remote_copy(
            src_ref=ybuf.at[:, z_of(by)], dst_ref=g0.at[slot_of(by)],
            send_sem=a2a_send.at[1], recv_sem=a2a_recv.at[part_of(by)],
            device_id=z_dev(by), device_id_type=MESH,
        ).start()
    here.start()

    def factors_here(level):
        for g, (lo, _) in enumerate(groups):
            if lo == level:
                for sem, side in ((loc_sem, core), (frecv_sem, 1 - core)):
                    three = fraw.at[:, lo : groups[g][1], side]
                    pltpu.make_async_copy(three, three, sem.at[g]).wait()

    def columns(f, level, slot):
        at = pl.multiple_of(lax.rem(x + NX - ORDER[slot], NX) * R, R)
        return fraw[f, level, :, :, pl.ds(at, R)].reshape(R, R)

    def prepare(level):
        factors_here(level)
        for f in range(3):
            for rel in range(NX):
                v = columns(f, level, rel)
                hi = v.astype(BF16)
                fhi[level, f * R : (f + 1) * R, rel * R : (rel + 1) * R] = hi
                flo[level, f * R : (f + 1) * R, rel * R : (rel + 1) * R] = (v - hi.astype(F32)).astype(BF16)

    def low(v):
        return lax.broadcasted_iota(jnp.int32, v.shape, 1) < dev_rows

    def turn_lanes(v):
        return pltpu.roll(v, dev_rows, 1)

    def firsts(a, b):
        return jnp.where(low(a), a, turn_lanes(b))

    def seconds(a, b):
        return jnp.where(low(a), turn_lanes(a), b)

    def prepare_first():
        factors_here(0)
        for f in range(3):
            for k in range(NX // 2):
                a, b = columns(f, 0, 2 * k), columns(f, 0, 2 * k + 1)
                v = jnp.where(core == 0, firsts(a, b), seconds(a, b))
                hi = v.astype(BF16)
                f0hi[f * R : (f + 1) * R, k * R : (k + 1) * R] = hi
                f0lo[f * R : (f + 1) * R, k * R : (k + 1) * R] = (v - hi.astype(F32)).astype(BF16)

    route = ((1, across), (2, right), (3, left))

    def chunk(level, t, slot):
        if level < 2:
            return GN.at[level, t, slot]
        return G2.at[t, slot] if level == 2 else G.at[level - 3, t, slot]

    def hop(level, t, k, piece=None):
        slot, dev = route[k]
        source, target, recv = chunk(level, t, 0), chunk(level, t, slot), ag_recv.at[level % 2, t, k]
        if piece is not None:
            some = pl.ds(piece * (Qs // 2), Qs // 2)
            source, target, recv = source.at[some], target.at[some], ag_recv.at[0, 2 * t + piece, k]
        return pltpu.make_async_remote_copy(
            src_ref=source, dst_ref=target, send_sem=ag_send.at[level % 2, t], recv_sem=recv,
            device_id=dev, device_id_type=MESH,
        )

    def send(level, t, piece=None):
        if level >= 2 and piece != 1:
            if level >= 5 or t < 2:
                sent(level - 2, t)
        for k in range(3):
            hop(level, t, k, piece).start()

    def arrived(level, t, k):
        if level == 2:
            for piece in range(2):
                hop(level, t, k, piece).wait_recv()
        else:
            hop(level, t, k).wait_recv()

    def sent(level, t):
        part = chunk(level, t, pl.ds(0, 3))
        pltpu.make_async_copy(part, part, ag_send.at[level % 2, t]).wait()

    def place(v, start, count):
        at = lax.broadcasted_iota(jnp.int32, v.shape, 0) + start
        return jnp.where(at >= count, at - count, at)

    def rolled(v, by):
        n = v.shape[0]
        if by % 8 or not by < n:
            return pltpu.roll(v, by % n, 0)
        return jnp.concatenate((v[n - by :], v[: n - by]), axis=0)

    def below(v, by, start, count):
        return jnp.where(place(v, start, count) < by, 0.0, rolled(v, by))

    def above(v, by, start, count):
        return jnp.where(place(v, start, count) >= count - by, 0.0, rolled(v, v.shape[0] - by))

    prepare_first()
    begins = [lax.rem(offset + t * Qs + Q - HALO, Q) for t in range(2)]
    for t in range(2):
        if t == 0:
            landed(1, g0.at[pl.ds(0, near_n)])
        elif near_n < nz:
            landed(2, g0.at[pl.ds(near_n, nz - near_n)])
        for i in range(Qh // n_half):
            c = (t * Qs - HALO) // n_half + i
            GN[0, t, 0, i * n_half : (i + 1) * n_half, :] = g0[(c // NY + 1) % nz, c % NY]
        send(0, t)
    prepare(1)
    for t in range(2):
        for k in (1, 2, 0):
            arrived(0, t, k)
        a = [GN[0, t, rel] for rel in range(NX)]
        ev = jnp.concatenate((firsts(a[0], a[1]), firsts(a[2], a[3])), axis=1)
        pe = three_pass(ev, f0hi[...], f0lo[...])
        od = jnp.concatenate((seconds(a[0], a[1]), seconds(a[2], a[3])), axis=1)
        po = three_pass(od, f0hi[...], f0lo[...])
        to_even = pe[:, :R] - below(po[:, R : 2 * R], 1, begins[t], Q) - po[:, 2 * R :]
        to_odd = po[:, :R] - pe[:, R : 2 * R] - above(pe[:, 2 * R :], 1, begins[t], Q)
        hs[t] = jnp.where(core == 0, to_odd, to_even)
        pair_copy(t, hs.at[t], hx.at[t]).start()
        GN[1, t, 0] = jnp.where(core == 0, to_even, to_odd)

        def joined(t=t):
            pair_copy(t, hs.at[t], hx.at[t]).wait_recv()
            GN[1, t, 0] = GN[1, t, 0] + hx[t]
            send(1, t)

        if t == 0:
            waiting = joined
            pl.when(core == 0)(joined)
        else:
            pl.when(core == 1)(waiting)
            joined()

    prepare(2)
    for t in range(2):
        arrived(1, t, 0)
        v = jnp.concatenate((GN[1, t, 0], GN[1, t, 1]), axis=1)
        first_half[...] = three_pass(v, fhi[1, :, : 2 * R], flo[1, :, : 2 * R])
        arrived(1, t, 1)
        arrived(1, t, 2)
        v = jnp.concatenate((GN[1, t, 2], GN[1, t, 3]), axis=1)
        p = first_half[...] + three_pass(v, fhi[1, :, 2 * R :], flo[1, :, 2 * R :])
        new = p[:, :R] - below(p[:, R : 2 * R], 1, begins[t], Q) - above(p[:, 2 * R :], 1, begins[t], Q)
        obuf[t] = new[HALO : HALO + Qs]
        for u in range(2):
            G2[u, 0, t * (Qs // 2) : (t + 1) * (Qs // 2), :] = obuf[t, pl.ds(u, Qs // 2, stride=2), :]
            send(2, u, t)

    def part(level, t, first):
        n, base = (Qs, 4) if level == 2 else (Qs // 2, 0)
        for slot in (first, first + 1):
            if slot == 0 and level > 2:
                continue
            v = chunk(level, t, slot)[...]
            hi = v.astype(BF16)
            both[t + base, :n, slot * R : (slot + 1) * R] = hi
            both[t + base, n : 2 * n, slot * R : (slot + 1) * R] = (v - hi.astype(F32)).astype(BF16)
        ks = slice(first * R, (first + 2) * R)
        p = dot_t(both[t + base, : 2 * n, ks], fhi[level, :, ks])
        return p[:n] + p[n:] + dot_t(both[t + base, :n, ks], flo[level, :, ks])

    def finish(level, t):
        n = Qs if level == 2 else Qs // 2
        arrived(level, t, 0)
        prod[t, :n] = part(level, t, 0)
        arrived(level, t, 1)
        arrived(level, t, 2)
        p = prod[t, :n] + part(level, t, 2)
        by = 2 ** (level - (2 if level == 2 else 3))
        start = offset // (Q // n)
        return p[:, :R] - below(p[:, R : 2 * R], by, start, n) - above(p[:, 2 * R :], by, start, n)

    def own_chunk(level, w, v):
        G[level - 3, w, 0] = v
        send(level, w)
        hi = v.astype(BF16)
        both[w, : Qs // 2, :R] = hi
        both[w, Qs // 2 : Qs, :R] = (v - hi.astype(F32)).astype(BF16)

    prepare(3)
    for t in range(2):
        obuf[t] = finish(2, t)
        for u in range(2):
            own_chunk(3, 2 * t + u, obuf[t, pl.ds(u, Qs // 2, stride=2), :])

    for level in range(3, levels - 1):
        prepare(level + 1)
        for w in range(4):
            own_chunk(level + 1, w, finish(level, w))

    def swapped(w):
        pair_copy(2 + w, es.at[w], ex.at[w]).wait_recv()
        new, got = es[w], turn_lanes(ex[w])
        packed = jnp.where(low(new) == (core == 0), new, got)
        for cz in range(nz):
            back[w, cz, :, 0, :] = packed[cz * NY : (cz + 1) * NY]
        home(w)

    def home(t):
        own = pltpu.make_async_copy(back.at[t, zsh, y], bdst.at[t, y, z], a2a_recv.at[3 + t])
        for bz in range(nz // 2, -1, -1):
            for dz in both_ways(bz) if bz else (0,):
                for dy in range(NY):
                    if dz or dy:
                        pltpu.make_async_remote_copy(
                            src_ref=back.at[t, (zsh + dz) % nz, y_of(dy)], dst_ref=bdst.at[t, y, z],
                            send_sem=a2a_send.at[2], recv_sem=a2a_recv.at[3 + t],
                            device_id=(z_of(dz) * NY + y_of(dy), rows), device_id_type=MESH,
                        ).start()
        own.start()

    for w in range(4):
        es[w] = finish(levels - 1, w)
        pair_copy(2 + w, es.at[w], ex.at[w]).start()
        if w:
            swapped(w - 1)
    swapped(3)

    for level in (levels - 2, levels - 1):
        for t in range(4):
            sent(level, t)
    for g, (lo, hi) in enumerate(groups):
        three = fraw.at[:, lo:hi, core]
        pltpu.make_async_copy(three, three, fsend_sem.at[g]).wait()
    gone(0, src.at[:, pl.ds(0, NY - 1)])
    gone(1, ybuf.at[:, pl.ds(0, nz - 1)])
    for k, source in enumerate((hs, es)):
        pltpu.make_async_copy(source, source, pair_send.at[k]).wait()
    for w in range(4):
        landed(3 + w, bdst.at[w])
        m = 2 * (w % 2) + w // 2
        for cy in range(NY):
            turn[m, pl.ds(cy, nz, stride=NY), :] = bdst[w, cy, :, 0, :]
        wide = jnp.transpose(turn[m])
        out[:, m * 2 * C : (m + 1) * 2 * C] = jnp.concatenate((wide[:dev_rows], wide[dev_rows:]), axis=1)
    gone(2, zbuf)


def solution(mesh):
    n_chain, n_rows = mesh.shape["chain"], mesh.shape["rows"]
    assert n_rows == 2 * NX and n_chain % NY == 0

    def on_device(rhs, diag, left_f, right_f):
        levels, dev_rows, M = diag.shape
        n_half = rhs.shape[1] // n_chain // 2
        C, R = n_chain, 2 * dev_rows
        nz = C // NY
        Q = C * n_half
        Qs = Q // 2
        Qh = Qs + 2 * HALO
        groups = ((0, 1), (1, 3), (3, levels))
        scratch = [
            pltpu.VMEM(rhs.shape, F32),
            pltpu.VMEM((nz, NY, n_half, R), F32),
            pltpu.VMEM((NY, nz, n_half, R), F32),
            pltpu.VMEM((nz, NY, n_half, R), F32),
            pltpu.VMEM((2, 2, NX, Qh, R), F32),
            pltpu.VMEM((2, NX, Qs, R), F32),
            pltpu.VMEM((levels - 3, 4, NX, Qs // 2, R), F32),
            pltpu.VMEM((3, levels, 2, dev_rows, M), F32),
            pltpu.VMEM((3 * R, M // 2), BF16),
            pltpu.VMEM((3 * R, M // 2), BF16),
            pltpu.VMEM((levels, 3 * R, M), BF16),
            pltpu.VMEM((levels, 3 * R, M), BF16),
            pltpu.VMEM((6, 2 * Qs, M), BF16),
            pltpu.VMEM((4, Qs, 3 * R), F32),
            pltpu.VMEM((Qh, 3 * R), F32),
            pltpu.VMEM((2, Qh, R), F32),
            pltpu.VMEM((2, Qh, R), F32),
            pltpu.VMEM((2, Qs, R), F32),
            pltpu.VMEM((4, Qs // 2, R), F32),
            pltpu.VMEM((4, Qs // 2, R), F32),
            pltpu.VMEM((4, nz, NY, 1, R), F32),
            pltpu.VMEM((4, C - 1, 1, R), F32),
            pltpu.VMEM((4, NY, nz, 1, R), F32),
            pltpu.VMEM((n_half, C, R), F32),
            pltpu.SemaphoreType.DMA((len(groups),)),
            pltpu.SemaphoreType.DMA((len(groups),)),
            pltpu.SemaphoreType.DMA((len(groups),)),
            pltpu.SemaphoreType.DMA((2,)),
            pltpu.SemaphoreType.DMA((6,)),
            pltpu.SemaphoreType.DMA((3,)),
            pltpu.SemaphoreType.DMA((7,)),
            pltpu.SemaphoreType.DMA((2, 4)),
            pltpu.SemaphoreType.DMA((2, 4, 3)),
            pltpu.SemaphoreType.DMA,
            pltpu.SemaphoreType.REGULAR,
        ]
        vm = pl.BlockSpec(memory_space=pltpu.VMEM)
        hbm = pl.BlockSpec(memory_space=pl.ANY)
        return pl.pallas_call(
            functools.partial(kernel, n_chain, levels, groups),
            out_shape=jax.ShapeDtypeStruct(rhs.shape, F32),
            in_specs=[hbm, hbm, hbm, hbm],
            out_specs=vm,
            scratch_shapes=scratch,
            compiler_params=pltpu.CompilerParams(
                collective_id=0, has_side_effects=True, vmem_limit_bytes=215 * 2**18
            ),
        )(rhs, diag, left_f, right_f)

    placed = (
        P("rows", "chain"),
        P(None, "rows", None),
        P(None, "rows", None),
        P(None, "rows", None),
    )
    return jax.shard_map(
        on_device, mesh=mesh, in_specs=placed, out_specs=P("rows", "chain"), check_vma=False
    )
```
